256 devices in a mesh: outer: 8 (over y, x_lo), inner: 32 (over z, x_hi, core).
Axes of the slice: x: 4 (x_hi: 2, x_lo: 2; x = x_hi * 2 + x_lo), y: 4, z: 8, core: 2. Of those that a mesh axis runs over, the one named last changes fastest.
Arguments:
- patches: bfloat16 [65536, 1536], P(('outer', 'inner')), may hold values from -6 to 6
- stem_weight: bfloat16 [1536, 1024], replicated, may hold values from -0.15625 to 0.15625
- ln_gain: float32 [1024], replicated, may hold values from 0.1 to 1.9
- up_weight: bfloat16 [1024, 2048], replicated, may hold values from -0.1875 to 0.1875
- down_weight: bfloat16 [2048, 1024], replicated, may hold values from -0.125 to 0.125
- cotangent: bfloat16 [65536, 1024], P(('outer', 'inner')), may hold values from -0.0234375 to 0.0234375
Outputs:
- grad_stem: float32 [1536, 1024], P('inner')
- grad_up: float32 [1024, 2048], P('inner')
- grad_down: float32 [2048, 1024], P('inner')
The draws below stay inside these ranges and needn't reach their ends.
All inputs are finite; a program needn't handle non-finite values.
Results may differ from the reference program's by a relative error of at most 0.025.
Values may be sent and summed in bfloat16 or wider, within the bound.
No kernel may reach another device: no remote copies, remote signals or barrier semaphores. Data moves between devices by JAX's collectives and lax.ppermute only.
A program may use at most 128 MiB of HBM per device.

```python
import math
import jax
import jax.numpy as jnp
from jax import lax

D = 1024
FF = 2048
P_SIZE = 1536
TOK_DEV = 256
TOKENS = 65536


def levels(key, extent, split, low, top_value):
    def one(dim, parts):
        steps = jax.random.uniform(jax.random.fold_in(jax.random.fold_in(key, 6), dim), (parts,), jnp.float32, low / len(split), top_value / len(split))
        return jnp.repeat(jnp.exp(steps), extent[dim] // parts).reshape((-1,) + (1,) * (len(extent) - dim - 1))

    level = one(*split[0])
    for cut in split[1:]:
        level = level * one(*cut)
    return level


def scatter_about(rng, shape, deviation, bound, split=(), dtype=jnp.bfloat16):
    values = deviation * jax.random.normal(rng, shape, jnp.float32)
    if split:
        values = values * levels(rng, shape, split, -0.22, 0.18)
    return jnp.clip(values, -bound, bound).astype(dtype)


def setup_inputs(seed: int = 0) -> dict:
    keys = jax.random.split(jax.random.key(seed), 7)
    return {
        "patches": scatter_about(keys[0], (TOKENS, P_SIZE), 1.0, 6.0, ((0, 256),)),
        "stem_weight": scatter_about(keys[1], (P_SIZE, D), P_SIZE ** -0.5, 0.15625),
        "ln_gain": jnp.clip(1.0 + 0.18 * jax.random.normal(keys[2], (D,), jnp.float32), 0.1, 1.9),
        "up_weight": scatter_about(keys[3], (D, FF), D ** -0.5, 0.1875),
        "down_weight": scatter_about(keys[4], (FF, D), FF ** -0.5, 0.125),
        "cotangent": scatter_about(keys[5], (TOKENS, D), (TOKENS ** -0.5), 0.0234375, ((0, 256),)),
    }


def block_grads(patches, stem_weight, ln_gain, up_weight, down_weight, cotangent):
    embed = jnp.dot(patches, stem_weight, preferred_element_type=jnp.float32).astype(jnp.bfloat16)
    embed_f = embed.astype(jnp.float32)
    center = lax.optimization_barrier(jnp.mean(embed_f, axis=1, keepdims=True))
    shifted = embed_f - center
    inverse = lax.rsqrt(lax.optimization_barrier(jnp.mean(shifted * shifted, axis=1, keepdims=True)) + 1e-06)
    normal = shifted * inverse
    normed = (normal * ln_gain).astype(jnp.bfloat16)
    preact = jnp.dot(normed, up_weight, preferred_element_type=jnp.float32)
    hidden = jax.nn.gelu(preact, approximate=False).astype(jnp.bfloat16)
    over_rows = (((0,), (0,)), ((), ()))
    over_cols = (((1,), (1,)), ((), ()))
    grad_down = lax.dot_general(hidden, cotangent, over_rows, preferred_element_type=jnp.float32)
    hidden_grad = lax.dot_general(cotangent, down_weight, over_cols, preferred_element_type=jnp.float32)
    derivative = 0.5 * (1.0 + jax.scipy.special.erf(preact / math.sqrt(2.0))) + preact * jnp.exp(-0.5 * preact * preact) / math.sqrt(2.0 * math.pi)
    preact_grad = (hidden_grad * derivative).astype(jnp.bfloat16)
    grad_up = lax.dot_general(normed, preact_grad, over_rows, preferred_element_type=jnp.float32)
    normal_grad = lax.dot_general(preact_grad, up_weight, over_cols, preferred_element_type=jnp.float32) * ln_gain
    first_mean = lax.optimization_barrier(jnp.mean(normal_grad, axis=1, keepdims=True))
    second_mean = lax.optimization_barrier(jnp.mean(normal_grad * normal, axis=1, keepdims=True))
    embed_grad = (cotangent.astype(jnp.float32) + inverse * (normal_grad - first_mean - normal * second_mean)).astype(jnp.bfloat16)
    grad_stem = lax.dot_general(patches, embed_grad, over_rows, preferred_element_type=jnp.float32)
    return (grad_stem.astype(jnp.bfloat16), grad_up.astype(jnp.bfloat16), grad_down.astype(jnp.bfloat16))

def widen(term):
    return lax.optimization_barrier(term).astype(jnp.float32)

def reference(patches, stem_weight, ln_gain, up_weight, down_weight, cotangent):
    blocks = TOKENS // TOK_DEV
    patch_blocks = patches.reshape(blocks, TOK_DEV, P_SIZE)
    cot_blocks = cotangent.reshape(blocks, TOK_DEV, D)

    def accumulate(carry, pieces):
        terms = block_grads(pieces[0], stem_weight, ln_gain, up_weight, down_weight, pieces[1])
        return ((carry[0] + widen(terms[0]), carry[1] + widen(terms[1]), carry[2] + widen(terms[2])), None)
    start = (jnp.zeros((P_SIZE, D), jnp.float32), jnp.zeros((D, FF), jnp.float32), jnp.zeros((FF, D), jnp.float32))
    totals, unused = lax.scan(accumulate, start, (patch_blocks, cot_blocks))
    return (totals[0], totals[1], totals[2])
```

```python
import functools
import math

import jax
import jax.numpy as jnp
from jax import lax
from jax.experimental import pallas as pl
from jax.experimental.pallas import tpu as pltpu
from jax.sharding import PartitionSpec as P

BF = jnp.bfloat16
F32 = jnp.float32
AXES = ("outer", "inner")
VMEM = pl.BlockSpec(memory_space=pltpu.VMEM)
SMEM = pl.BlockSpec(memory_space=pltpu.SMEM)
LANES = 128


def move(value, dx=0, dy=0, dz=0, dc=0, dxl=0):
    pairs = []
    for y in range(4):
        for x in range(4):
            for z in range(8):
                for c in range(2):
                    X, Y, Z, C = (x + dx) % 4, (y + dy) % 4, (z + dz) % 8, (c + dc) % 2
                    X = (X // 2) * 2 + (X % 2 + dxl) % 2
                    src = (y * 2 + x % 2) * 32 + z * 4 + (x // 2) * 2 + c
                    dst = (Y * 2 + X % 2) * 32 + Z * 4 + (X // 2) * 2 + C
                    pairs.append((src, dst))
    return lax.ppermute(value, AXES, sorted(pairs))


def call(body, outs, scratch, name, *operands, limit=40):
    specs = [SMEM] + [VMEM] * (len(operands) - 1)
    return pl.pallas_call(
        body,
        out_shape=[jax.ShapeDtypeStruct(s, d) for s, d in outs],
        in_specs=specs,
        out_specs=[VMEM] * len(outs),
        scratch_shapes=scratch,
        name=name,
        compiler_params=pltpu.CompilerParams(vmem_limit_bytes=limit << 20),
    )(*operands)


def split_body(rr, pos, x_ref, mine, send, t_ref):
    c = pos[3]
    t = x_ref[...].T
    for b in range(16):
        for half in range(2):
            at = (b * 2 + half) * rr
            t_ref[b, half] = t[at : at + rr]
    mine[...] = t_ref[:, c]
    send[...] = t_ref[:, 1 - c]


def split_transposed(pos, x, rr):
    tokens = x.shape[0]
    outs = [((16, rr, tokens), BF)] * 2
    return call(
        functools.partial(split_body, rr),
        outs,
        [pltpu.VMEM((16, 2, rr, tokens), BF)],
        "split_transposed",
        pos,
        x,
    )


def place(rel, outs):
    mp, mm, kp, ow = outs
    return {
        0: (ow.at[0], ow.at[1]),
        1: (kp.at[0], mp.at[1]),
        2: (mp.at[0], mm.at[0]),
        3: (mm.at[1], kp.at[1]),
    }[rel]


def term_body(kind, first, z0, nz, rr, pos, lm, lr, rm, rv, *outs):
    x, y = pos[0], pos[1]

    def columns(ref, starts, width):
        return jnp.concatenate(
            [ref[:, pl.ds(pl.multiple_of(s, LANES), width)] for s in starts], axis=1
        )

    for rel in range(4):
        if first == "x":
            to = lax.rem(x + rel, 4)
            xh, xl = to // 2, lax.rem(to, 2)
            left = [ref[z0 : z0 + 2 * nz, xh].reshape(2 * nz * rr, -1) for ref in (lm, lr)]
            if kind == "up":
                starts, width = [(yy * 2 + xl) * 256 for yy in range(4)], 256
            else:
                starts, width = [xl * 512], 512
        else:
            to = lax.rem(y + rel, 4)
            left = [ref[z0 : z0 + 2 * nz].reshape(2 * nz * 2 * rr, -1) for ref in (lm, lr)]
            if kind == "up":
                starts, width = [to * 512], 512
            else:
                starts, width = [to * 128, 512 + to * 128], 128
        acc = jnp.dot(left[0], columns(rm, starts, width), preferred_element_type=F32)
        acc += jnp.dot(left[1], columns(rv, starts, width), preferred_element_type=F32)
        acc = acc.astype(BF)
        dests = place(rel, outs)
        parts = 2 if kind == "up" else 1
        for zi in range(2 * nz):
            dst = dests[zi // nz]
            for other in range(4):
                for k in range(parts):
                    if first == "x":
                        row = zi * rr
                        col = (other * parts + k) * LANES
                    else:
                        row = (zi * 2 + other // 2) * rr
                        col = ((other % 2) * parts + k) * LANES
                    dst[other, zi % nz, k * rr : (k + 1) * rr] = acc[
                        row : row + rr, col : col + LANES
                    ]


def terms(pos, kind, first, z0, nz, left, right):
    rr = left[0].shape[1]
    rows = rr * (2 if kind == "up" else 1)
    lm, lr = (v.reshape(8, 2, rr, v.shape[-1]) for v in left)
    outs = [((2, 4, nz, rows, LANES), BF)] * 4
    return call(
        functools.partial(term_body, kind, first, z0, nz, rr),
        outs,
        [],
        "terms_" + kind,
        pos,
        lm,
        lr,
        right[0],
        right[1],
    )


def forward_body(kp, r1, r2, s1, s2):
    s1[...] = (kp[0].astype(F32) + r1[0].astype(F32)).astype(BF)
    s2[...] = (kp[1].astype(F32) + r2[0].astype(F32)).astype(BF)


def ring(axis, mp, mm, kp):
    step = functools.partial(move, **{"d" + axis: 1})
    back = functools.partial(move, **{"d" + axis: -1})
    r1 = step(mp)
    r2 = back(mm)
    s1, s2 = pl.pallas_call(
        forward_body,
        out_shape=[jax.ShapeDtypeStruct(kp.shape[1:], BF)] * 2,
        in_specs=[VMEM] * 3,
        out_specs=[VMEM] * 2,
        name="ring_forward",
        compiler_params=pltpu.CompilerParams(vmem_limit_bytes=32 << 20),
    )(kp, r1, r2)
    return r1, r2, step(s1), back(s2)


def add3(a, b, c):
    return a.astype(F32) + b.astype(F32) + c.astype(F32)


def between_body(second, pos, ow, r1, r2, q1, q2, *outs):
    me = pos[0] if second == "x" else pos[1]
    for rel in range(4):
        to = lax.rem(me + rel, 4)
        da, db = place(rel, outs)
        da[...] = add3(ow[0, to], r2[1, to], q1[to]).astype(BF)
        db[...] = add3(ow[1, to], r1[1, to], q2[to]).astype(BF)


def reduce_xy(pos, first, pieces):
    second = "y" if first == "x" else "x"
    mp, mm, kp, ow = pieces
    r1, r2, q1, q2 = ring(first, mp, mm, kp)
    outs = [((2,) + tuple(ow.shape[2:]), BF)] * 4
    mp, mm, kp, ow = call(
        functools.partial(between_body, second), outs, [], "ring_turn", pos, ow, r1, r2, q1, q2
    )
    r1, r2, q1, q2 = ring(second, mp, mm, kp)
    return ow, r1, r2, q1, q2


ROWS = 176


def pack_body(layout, pos, *refs):
    z = pos[2]
    ins, outs, buf = refs[: 5 * len(layout)], refs[5 * len(layout) : -1], refs[-1]
    for p, (z0, nz, base, rows) in enumerate(layout):
        ow, r1, r2, q1, q2 = ins[5 * p : 5 * p + 5]
        buf[z0 : z0 + nz, base : base + rows] = add3(ow[0], r2[1], q1[...]).astype(BF)
        buf[z0 + nz : z0 + 2 * nz, base : base + rows] = add3(ow[1], r1[1], q2[...]).astype(BF)
    for rel in range(8):
        outs[rel][...] = buf[lax.rem(z + rel, 8)]


def sum_body(*refs):
    total = refs[0][...].astype(F32)
    for ref in refs[1:-1]:
        total += ref[...].astype(F32)
    refs[-1][...] = total.astype(BF)


def unpack_body(pos, *refs):
    ins, (stem, up, down), buf = refs[:8], refs[8:11], refs[11]
    y, xl = pos[1], lax.rem(pos[0], 2)
    for dy in range(4):
        for dxl in range(2):
            at = lax.rem(y + 4 - dy, 4) * 2 + lax.rem(xl + dxl, 2)
            buf[at] = ins[dy * 2 + dxl][...].astype(F32)
    for yy in range(4):
        for ll in range(2):
            piece = buf.at[yy * 2 + ll]
            col = (ll * 4 + yy) * LANES
            down[:, col : col + LANES] = piece[0:64]
            stem[:, col : col + LANES] = piece[128:176]
            col = (yy * 2 + ll) * 256
            up[:, col : col + LANES] = piece[64:96]
            up[:, col + LANES : col + 256] = piece[96:128]


def finish(pos, layout, parts):
    flat = [ref for part in parts for ref in part]
    sends = call(
        functools.partial(pack_body, layout),
        [((ROWS, LANES), BF)] * 8,
        [pltpu.VMEM((8, ROWS, LANES), BF)],
        "z_pack",
        pos,
        *flat,
    )
    got = [sends[0]] + [move(sends[k], dz=k) for k in range(1, 8)]
    (share,) = pl.pallas_call(
        sum_body,
        out_shape=[jax.ShapeDtypeStruct((ROWS, LANES), BF)],
        in_specs=[VMEM] * 8,
        out_specs=[VMEM],
        name="z_sum",
    )(*got)
    every = []
    for dy in range(4):
        for dxl in range(2):
            every.append(share if dy + dxl == 0 else move(share, dy=dy, dxl=dxl))
    return call(
        unpack_body,
        [((48, 1024), F32), ((32, 2048), F32), ((64, 1024), F32)],
        [pltpu.VMEM((8, ROWS, LANES), F32)],
        "unpack",
        pos,
        *every,
    )


def local(patches, stem_weight, ln_gain, up_weight, down_weight, cotangent):
    outer, inner = lax.axis_index("outer"), lax.axis_index("inner")
    x = ((inner // 2) % 2) * 2 + outer % 2
    pos = jnp.stack([x, outer // 2, inner // 4, inner % 2]).astype(jnp.int32)

    cot_other = move(cotangent, dc=1)
    patches_mine, patches_send = split_transposed(pos, patches, 48)
    patches_other = move(patches_send, dc=1)

    embed = jnp.dot(patches, stem_weight, preferred_element_type=F32).astype(BF)
    embed_f = embed.astype(F32)
    center = jnp.mean(embed_f, axis=1, keepdims=True)
    shifted = embed_f - center
    inverse = lax.rsqrt(jnp.mean(shifted * shifted, axis=1, keepdims=True) + 1e-06)
    normal = shifted * inverse
    normed = (normal * ln_gain).astype(BF)
    normed_mine, normed_send = split_transposed(pos, normed, 32)
    normed_other = move(normed_send, dc=1)
    preact = jnp.dot(normed, up_weight, preferred_element_type=F32)
    hidden = jax.nn.gelu(preact, approximate=False).astype(BF)
    hidden_mine, hidden_send = split_transposed(pos, hidden, 64)
    hidden_other = move(hidden_send, dc=1)

    over_cols = (((1,), (1,)), ((), ()))
    hidden_grad = lax.dot_general(cotangent, down_weight, over_cols, preferred_element_type=F32)
    derivative = 0.5 * (1.0 + lax.erf(preact / math.sqrt(2.0))) + preact * jnp.exp(
        -0.5 * preact * preact
    ) / math.sqrt(2.0 * math.pi)
    preact_grad = (hidden_grad * derivative).astype(BF)
    preact_other = move(preact_grad, dc=1)

    down = terms(
        pos, "down", "x", 0, 4, (hidden_mine, hidden_other), (cotangent, cot_other)
    )
    down = reduce_xy(pos, "x", down)

    normal_grad = (
        lax.dot_general(preact_grad, up_weight, over_cols, preferred_element_type=F32) * ln_gain
    )
    first_mean = jnp.mean(normal_grad, axis=1, keepdims=True)
    second_mean = jnp.mean(normal_grad * normal, axis=1, keepdims=True)
    embed_grad = (
        cotangent.astype(F32) + inverse * (normal_grad - first_mean - normal * second_mean)
    ).astype(BF)
    embed_other = move(embed_grad, dc=1)

    up = terms(pos, "up", "y", 0, 4, (normed_mine, normed_other), (preact_grad, preact_other))
    up = reduce_xy(pos, "y", up)

    left, right = (patches_mine, patches_other), (embed_grad, embed_other)
    stem_x = reduce_xy(pos, "x", terms(pos, "stem", "x", 0, 2, left, right))
    stem_y = reduce_xy(pos, "y", terms(pos, "stem", "y", 4, 2, left, right))

    layout = ((0, 4, 0, 64), (0, 4, 64, 64), (0, 2, 128, 48), (4, 2, 128, 48))
    return tuple(finish(pos, layout, (down, up, stem_x, stem_y)))


def solution(mesh):
    in_specs = (P(AXES, None), P(), P(), P(), P(), P(AXES, None))
    out_specs = (P("inner", None), P("inner", None), P("inner", None))
    return jax.shard_map(local, mesh=mesh, in_specs=in_specs, out_specs=out_specs, check_vma=False)
```

```python
import functools
import math

import jax
import jax.numpy as jnp
from jax import lax
from jax.experimental import pallas as pl
from jax.experimental.pallas import tpu as pltpu
from jax.sharding import Mesh, PartitionSpec as P

BF = jnp.bfloat16
F32 = jnp.float32
AXES = ("y", "xl", "z", "xh", "c")
VMEM = pl.BlockSpec(memory_space=pltpu.VMEM)
SMEM = pl.BlockSpec(memory_space=pltpu.SMEM)
LANES = 128


def move(value, dx=0, dy=0, dc=0):
    pairs = []
    for y in range(4):
        for x in range(4):
            for z in range(8):
                for c in range(2):
                    X, Y, C = (x + dx) % 4, (y + dy) % 4, (c + dc) % 2
                    src = (y * 2 + x % 2) * 32 + z * 4 + (x // 2) * 2 + c
                    dst = (Y * 2 + X % 2) * 32 + z * 4 + (X // 2) * 2 + C
                    pairs.append((src, dst))
    return lax.ppermute(value, AXES, sorted(pairs))


def call(body, outs, scratch, name, *operands, limit=8):
    specs = [SMEM] + [VMEM] * (len(operands) - 1)
    return pl.pallas_call(
        body,
        out_shape=[jax.ShapeDtypeStruct(s, d) for s, d in outs],
        in_specs=specs,
        out_specs=[VMEM] * len(outs),
        scratch_shapes=scratch,
        name=name,
        compiler_params=pltpu.CompilerParams(vmem_limit_bytes=limit << 20),
    )(*operands)


def split_body(rr, pos, x_ref, mine, send, t_ref):
    c = pos[3]
    t = x_ref[...].T
    for b in range(16):
        for half in range(2):
            at = (b * 2 + half) * rr
            t_ref[b, half] = t[at : at + rr]
    mine[...] = t_ref[:, c]
    send[...] = t_ref[:, 1 - c]


def split_transposed(pos, x, rr):
    tokens = x.shape[0]
    outs = [((16, rr, tokens), BF)] * 2
    return call(
        functools.partial(split_body, rr),
        outs,
        [pltpu.VMEM((16, 2, rr, tokens), BF)],
        "split_transposed",
        pos,
        x,
        limit=12,
    )


ROWS = 176
HALF = 352


def place(rel, outs):
    mp, mm, kp, ow = outs
    return {
        0: (ow.at[0], ow.at[1]),
        1: (kp.at[0], mp.at[1]),
        2: (mp.at[0], mm.at[0]),
        3: (mm.at[1], kp.at[1]),
    }[rel]


def dot2(lefts, rights):
    acc = jnp.dot(lefts[0], rights[0], preferred_element_type=F32)
    acc += jnp.dot(lefts[1], rights[1], preferred_element_type=F32)
    return acc.astype(BF)


def terms_body(pos, hm, hr, nm, nr, pm, pr, cm, cr, gm, gr, em, er, *outs):
    x, y = pos[0], pos[1]

    def columns(ref, start, width):
        return ref[:, pl.ds(pl.multiple_of(start, LANES), width)]

    for rel in range(4):
        to = lax.rem(x + rel, 4)
        xh, xl = to // 2, lax.rem(to, 2)
        dests = place(rel, outs[:4])
        acc = dot2(
            [ref[:, xh].reshape(512, 256) for ref in (hm, hr)],
            [columns(ref, xl * 512, 512) for ref in (cm, cr)],
        )
        for z in range(8):
            for yy in range(4):
                dests[z // 4][yy, z % 4 * 64 : z % 4 * 64 + 64] = acc[
                    z * 64 : z * 64 + 64, yy * 128 : yy * 128 + 128
                ]
        acc = dot2(
            [
                jnp.concatenate(
                    [ref[0:2, xh].reshape(96, 256), ref[4:6, xh].reshape(96, 256)], axis=0
                )
                for ref in (pm, pr)
            ],
            [columns(ref, xl * 512, 512) for ref in (em, er)],
        )
        for half in range(2):
            for yy in range(4):
                dests[half][yy, 256:352] = acc[
                    half * 96 : half * 96 + 96, yy * 128 : yy * 128 + 128
                ]
    for rel in range(4):
        to = lax.rem(y + rel, 4)
        dests = place(rel, outs[4:])
        acc = dot2(
            [ref[...].reshape(512, 256) for ref in (nm, nr)],
            [columns(ref, to * 512, 512) for ref in (gm, gr)],
        )
        for z in range(8):
            for xx in range(4):
                for k in range(2):
                    row, col = (z * 2 + xx // 2) * 32, (xx % 2 * 2 + k) * 128
                    at = z % 4 * 64 + k * 32
                    dests[z // 4][xx, at : at + 32] = acc[row : row + 32, col : col + 128]
        acc = dot2(
            [
                jnp.concatenate(
                    [ref[2:4].reshape(192, 256), ref[6:8].reshape(192, 256)], axis=0
                )
                for ref in (pm, pr)
            ],
            [
                jnp.concatenate(
                    [columns(ref, to * 128, 128), columns(ref, 512 + to * 128, 128)], axis=1
                )
                for ref in (em, er)
            ],
        )
        for half in range(2):
            for zi in range(2):
                for xx in range(4):
                    row, col = ((half * 2 + zi) * 2 + xx // 2) * 48, xx % 2 * 128
                    at = 256 + zi * 48
                    dests[half][xx, at : at + 48] = acc[row : row + 48, col : col + 128]


def terms(pos, hidden, normed, patches, cotangent, preact_grad, embed_grad):
    lefts = [v.reshape(8, 2, v.shape[1], v.shape[2]) for v in (*hidden, *normed, *patches)]
    outs = call(
        terms_body,
        [((2, 4, HALF, LANES), BF)] * 8,
        [],
        "terms",
        pos,
        *lefts,
        *cotangent,
        *preact_grad,
        *embed_grad,
        limit=24,
    )
    return outs[:4], outs[4:]


def forward_body(*refs):
    for p in range(2):
        kp, r1, r2 = refs[3 * p : 3 * p + 3]
        s1, s2 = refs[6 + 2 * p : 8 + 2 * p]
        s1[...] = (kp[0].astype(F32) + r1[0].astype(F32)).astype(BF)
        s2[...] = (kp[1].astype(F32) + r2[0].astype(F32)).astype(BF)


def rings(axes, parts):
    arrived = []
    for axis, (mp, mm, kp, ow) in zip(axes, parts):
        arrived.append((move(mp, **{"d" + axis: 1}), move(mm, **{"d" + axis: -1})))
    flat = [v for (r1, r2), part in zip(arrived, parts) for v in (part[2], r1, r2)]
    sums = pl.pallas_call(
        forward_body,
        out_shape=[jax.ShapeDtypeStruct(flat[0].shape[1:], BF)] * 4,
        in_specs=[VMEM] * 6,
        out_specs=[VMEM] * 4,
        name="ring_forward",
        compiler_params=pltpu.CompilerParams(vmem_limit_bytes=8 << 20),
    )(*flat)
    result = []
    for p, (axis, part) in enumerate(zip(axes, parts)):
        q1 = move(sums[2 * p], **{"d" + axis: 1})
        q2 = move(sums[2 * p + 1], **{"d" + axis: -1})
        result.append((part[3], *arrived[p], q1, q2))
    return result


def add3(a, b, c):
    return (a.astype(F32) + b.astype(F32) + c.astype(F32)).astype(BF)


def turn_body(pos, *refs):
    for p in range(2):
        ow, r1, r2, q1, q2 = refs[5 * p : 5 * p + 5]
        outs = refs[10 + 4 * p : 14 + 4 * p]
        me = pos[1 - p]
        for rel in range(4):
            to = lax.rem(me + rel, 4)
            da, db = place(rel, outs)
            da[...] = add3(ow[0, to], r2[1, to], q1[to])
            db[...] = add3(ow[1, to], r1[1, to], q2[to])


def reduce_xy(pos, parts):
    flat = [v for part in rings("xy", parts) for v in part]
    outs = call(turn_body, [((2, HALF, LANES), BF)] * 8, [], "ring_turn", pos, *flat)
    return [v for part in rings("yx", (outs[:4], outs[4:])) for v in part]


def pack_body(*refs):
    out = refs[10]
    for p in range(2):
        ow, r1, r2, q1, q2 = refs[5 * p : 5 * p + 5]
        halves = (add3(ow[0], r2[1], q1[...]), add3(ow[1], r1[1], q2[...]))
        for h, half in enumerate(halves):
            for zi in range(4):
                out[4 * h + zi, 64 * p : 64 * p + 64] = half[zi * 64 : zi * 64 + 64]
            for zi in range(2):
                out[4 * h + 2 * p + zi, 128:176] = half[256 + zi * 48 : 304 + zi * 48]


def sum_body(got, out):
    total = got[0].astype(F32)
    for k in range(1, 8):
        total += got[k].astype(F32)
    share = total.astype(BF)
    for k in range(8):
        out[k] = share


def unpack_body(got, stem, up, down):
    for y in range(4):
        for xl in range(2):
            piece = got[y * 2 + xl].astype(F32)
            col = (xl * 4 + y) * LANES
            down[:, col : col + LANES] = piece[0:64]
            stem[:, col : col + LANES] = piece[128:176]
            col = (y * 2 + xl) * 256
            up[:, col : col + LANES] = piece[64:96]
            up[:, col + LANES : col + 256] = piece[96:128]


def plain(body, outs, name, *operands):
    return pl.pallas_call(
        body,
        out_shape=[jax.ShapeDtypeStruct(s, d) for s, d in outs],
        in_specs=[VMEM] * len(operands),
        out_specs=[VMEM] * len(outs),
        name=name,
        compiler_params=pltpu.CompilerParams(vmem_limit_bytes=8 << 20),
    )(*operands)


def finish(pieces):
    share = [((8, ROWS, LANES), BF)]
    (packed,) = plain(pack_body, share, "z_pack", *pieces)
    got = lax.all_to_all(packed, "z", 0, 0, tiled=True)
    (copies,) = plain(sum_body, share, "z_sum", got)
    every = lax.all_to_all(copies, ("y", "xl"), 0, 0, tiled=True)
    outs = [((48, 1024), F32), ((32, 2048), F32), ((64, 1024), F32)]
    return plain(unpack_body, outs, "unpack", every)


def local(patches, stem_weight, ln_gain, up_weight, down_weight, cotangent):
    x = lax.axis_index("xh") * 2 + lax.axis_index("xl")
    pos = jnp.stack([x, lax.axis_index("y"), lax.axis_index("z"), lax.axis_index("c")])
    pos = pos.astype(jnp.int32)

    cot_other = move(cotangent, dc=1)
    patches_mine, patches_send = split_transposed(pos, patches, 48)
    patches_other = move(patches_send, dc=1)

    embed = jnp.dot(patches, stem_weight, preferred_element_type=F32).astype(BF)
    embed_f = embed.astype(F32)
    center = jnp.mean(embed_f, axis=1, keepdims=True)
    shifted = embed_f - center
    inverse = lax.rsqrt(jnp.mean(shifted * shifted, axis=1, keepdims=True) + 1e-06)
    normal = shifted * inverse
    normed = (normal * ln_gain).astype(BF)
    normed_mine, normed_send = split_transposed(pos, normed, 32)
    normed_other = move(normed_send, dc=1)
    preact = jnp.dot(normed, up_weight, preferred_element_type=F32)
    hidden = jax.nn.gelu(preact, approximate=False).astype(BF)
    hidden_mine, hidden_send = split_transposed(pos, hidden, 64)
    hidden_other = move(hidden_send, dc=1)

    over_cols = (((1,), (1,)), ((), ()))
    hidden_grad = lax.dot_general(cotangent, down_weight, over_cols, preferred_element_type=F32)
    derivative = 0.5 * (1.0 + lax.erf(preact / math.sqrt(2.0))) + preact * jnp.exp(
        -0.5 * preact * preact
    ) / math.sqrt(2.0 * math.pi)
    preact_grad = (hidden_grad * derivative).astype(BF)
    preact_other = move(preact_grad, dc=1)

    normal_grad = (
        lax.dot_general(preact_grad, up_weight, over_cols, preferred_element_type=F32) * ln_gain
    )
    first_mean = jnp.mean(normal_grad, axis=1, keepdims=True)
    second_mean = jnp.mean(normal_grad * normal, axis=1, keepdims=True)
    embed_grad = (
        cotangent.astype(F32) + inverse * (normal_grad - first_mean - normal * second_mean)
    ).astype(BF)
    embed_other = move(embed_grad, dc=1)

    parts = terms(
        pos,
        (hidden_mine, hidden_other),
        (normed_mine, normed_other),
        (patches_mine, patches_other),
        (cotangent, cot_other),
        (preact_grad, preact_other),
        (embed_grad, embed_other),
    )
    return tuple(finish(reduce_xy(pos, parts)))


def solution(mesh):
    fine = Mesh(mesh.devices.reshape(4, 2, 8, 2, 2), AXES)
    rows = P(("z", "xh", "c"), None)
    in_specs = (P(AXES, None), P(), P(), P(), P(), P(AXES, None))
    return jax.shard_map(
        local, mesh=fine, in_specs=in_specs, out_specs=(rows, rows, rows), check_vma=False
    )
```

```python
import functools
import math

import jax
import jax.numpy as jnp
from jax import lax
from jax.experimental import pallas as pl
from jax.experimental.pallas import tpu as pltpu
from jax.sharding import Mesh, PartitionSpec as P

BF = jnp.bfloat16
F32 = jnp.float32
AXES = ("y", "xl", "z", "xh", "c")
VMEM = pl.BlockSpec(memory_space=pltpu.VMEM)
SMEM = pl.BlockSpec(memory_space=pltpu.SMEM)
LANES = 128


def move(value, axis, hop):
    pairs = []
    for y in range(4):
        for x in range(4):
            for z in range(8):
                for c in range(2):
                    far = hop * (1 - 2 * c)
                    X = (x + far) % 4 if axis == "x" else x
                    Y = (y + far) % 4 if axis == "y" else y
                    C = 1 - c if axis == "c" else c
                    src = (y * 2 + x % 2) * 32 + z * 4 + (x // 2) * 2 + c
                    dst = (Y * 2 + X % 2) * 32 + z * 4 + (X // 2) * 2 + C
                    pairs.append((src, dst))
    return lax.ppermute(value, AXES, sorted(pairs))


def call(body, outs, scratch, name, *operands, limit=8, specs=None):
    return pl.pallas_call(
        body,
        out_shape=[jax.ShapeDtypeStruct(s, d) for s, d in outs],
        in_specs=specs or [SMEM] + [VMEM] * (len(operands) - 1),
        out_specs=[VMEM] * len(outs),
        scratch_shapes=scratch,
        name=name,
        compiler_params=pltpu.CompilerParams(vmem_limit_bytes=limit << 20),
    )(*operands)


SHARE = 144


def forward_pass_body(
    pos, gain, patches_any, stem_any, up_any, deriv, normal, inverse, mine, send, p, w, u, t, sem
):
    copies = [pltpu.make_async_copy(patches_any, p, sem.at[0])]
    for k in range(3):
        rows = pl.ds(k * 512, 512)
        copies.append(pltpu.make_async_copy(stem_any.at[rows], w.at[rows], sem.at[1 + k]))
    for k in range(2):
        cols = pl.ds(k * 1024, 1024)
        copies.append(pltpu.make_async_copy(up_any.at[:, cols], u.at[:, cols], sem.at[4 + k]))
    for copy in copies:
        copy.start()

    copies[0].wait()
    acc = None
    for k in range(3):
        copies[1 + k].wait()
        part = jnp.dot(
            p[:, k * 512 : k * 512 + 512], w[k * 512 : k * 512 + 512], preferred_element_type=F32
        )
        acc = part if acc is None else acc + part
    embed = acc.astype(BF).astype(F32)
    center = jnp.mean(embed, axis=1, keepdims=True)
    shifted = embed - center
    scale = lax.rsqrt(jnp.mean(shifted * shifted, axis=1, keepdims=True) + 1e-06)
    norm = shifted * scale
    normal[...] = norm
    inverse[...] = scale
    normed = (norm * gain[...]).astype(BF)
    pt = p[...].T
    nt = normed.T
    for b in range(16):
        for half in range(2):
            at = b * 2 + half
            t[b, half, 64:96] = nt[at * 32 : at * 32 + 32]
            t[b, half, 96:144] = pt[at * 48 : at * 48 + 48]
    for j in range(8):
        if j % 4 == 0:
            copies[4 + j // 4].wait()
        cols = slice(j * 256, j * 256 + 256)
        pre = jnp.dot(normed, u[:, cols], preferred_element_type=F32)
        cdf = 0.5 * (1.0 + lax.erf(pre * math.sqrt(0.5)))
        deriv[:, cols] = cdf + pre * jnp.exp(-0.5 * pre * pre) * (1.0 / math.sqrt(2.0 * math.pi))
        ht = (pre * cdf).astype(BF).T
        for q in range(4):
            t[j * 2 + q // 2, q % 2, 0:64] = ht[q * 64 : q * 64 + 64]
    c = pos[3]
    mine[...] = t[:, c]
    send[...] = t[:, 1 - c]


def forward_pass(pos, gain, patches, stem_weight, up_weight):
    anywhere = pl.BlockSpec(memory_space=pl.ANY)
    return call(
        forward_pass_body,
        [((256, 2048), F32), ((256, 1024), F32), ((256, 1), F32)] + [((16, SHARE, 256), BF)] * 2,
        [
            pltpu.VMEM((256, 1536), BF),
            pltpu.VMEM((1536, 1024), BF),
            pltpu.VMEM((1024, 2048), BF),
            pltpu.VMEM((16, 2, SHARE, 256), BF),
            pltpu.SemaphoreType.DMA((6,)),
        ],
        "forward_pass",
        pos,
        gain.reshape(1, 1024),
        patches,
        stem_weight,
        up_weight,
        limit=50,
        specs=[SMEM, VMEM, anywhere, anywhere, anywhere],
    )


ROWS = 176
CHUNK = 704


def chunk_of(me, pos, rel):
    return lax.rem(me + rel * (1 + 2 * pos[3]), 4)


def dot2(lefts, rights):
    acc = jnp.dot(lefts[0], rights[0], preferred_element_type=F32)
    acc += jnp.dot(lefts[1], rights[1], preferred_element_type=F32)
    return acc.astype(BF)


def terms_body(pos, lm, lr, cm, cr, gm, gr, em, er, *outs):
    def columns(ref, start, width):
        return ref[:, pl.ds(pl.multiple_of(start, LANES), width)]

    left = (lm, lr)
    for rel in range(4):
        to = chunk_of(pos[0], pos, rel)
        xh, xl = to // 2, lax.rem(to, 2)
        dst = outs[rel]
        acc = dot2(
            [ref[:, xh, 0:64].reshape(512, 256) for ref in left],
            [columns(ref, xl * 512, 512) for ref in (cm, cr)],
        )
        for yy in range(4):
            dst[yy, 0:512] = acc[:, yy * 128 : yy * 128 + 128]
        acc = dot2(
            [ref[0:4, xh, 96:144].reshape(192, 256) for ref in left],
            [columns(ref, xl * 512, 512) for ref in (em, er)],
        )
        for yy in range(4):
            dst[yy, 512:704] = acc[:, yy * 128 : yy * 128 + 128]
    for rel in range(4):
        to = chunk_of(pos[1], pos, rel)
        dst = outs[4 + rel]
        acc = dot2(
            [ref[:, :, 64:96].reshape(512, 256) for ref in left],
            [columns(ref, to * 512, 512) for ref in (gm, gr)],
        )
        for z in range(8):
            for xx in range(4):
                for k in range(2):
                    row, col = (z * 2 + xx // 2) * 32, (xx % 2 * 2 + k) * 128
                    at = z * 64 + k * 32
                    dst[xx, at : at + 32] = acc[row : row + 32, col : col + 128]
        acc = dot2(
            [ref[4:8, :, 96:144].reshape(384, 256) for ref in left],
            [
                jnp.concatenate(
                    [columns(ref, to * 128, 128), columns(ref, 512 + to * 128, 128)], axis=1
                )
                for ref in (em, er)
            ],
        )
        for z in range(4):
            for xx in range(4):
                row, col = (z * 2 + xx // 2) * 48, xx % 2 * 128
                at = 512 + z * 48
                dst[xx, at : at + 48] = acc[row : row + 48, col : col + 128]


def terms(pos, left, cotangent, preact_grad, embed_grad):
    outs = call(
        terms_body,
        [((4, CHUNK, LANES), BF)] * 8,
        [],
        "terms",
        pos,
        *[v.reshape(8, 2, SHARE, 256) for v in left],
        *cotangent,
        *preact_grad,
        *embed_grad,
        limit=24,
    )
    return outs[:4], outs[4:]


def pass_on_body(keep, got, out):
    out[...] = (keep[...].astype(F32) + got[...].astype(F32)).astype(BF)


def rings(axes, parts):
    result = []
    for axis, (own, keep, ahead, behind) in zip(axes, parts):
        got = move(ahead, axis, 1)
        near = move(behind, axis, -1)
        (total,) = call(
            pass_on_body, [(keep.shape, BF)], [], "pass_on", keep, got, specs=[VMEM, VMEM]
        )
        result += [own, near, move(total, axis, 1)]
    return result


def add3(a, b, c):
    return (a.astype(F32) + b.astype(F32) + c.astype(F32)).astype(BF)


def turn_body(pos, *refs):
    for p in range(2):
        a, b, c = refs[3 * p : 3 * p + 3]
        for rel in range(4):
            to = chunk_of(pos[1 - p], pos, rel)
            refs[6 + 4 * p + rel][...] = add3(a[to], b[to], c[to])


def reduce_xy(pos, parts):
    outs = call(
        turn_body, [((CHUNK, LANES), BF)] * 8, [], "ring_turn", pos, *rings("xy", parts)
    )
    return rings("yx", (outs[:4], outs[4:]))


def pack_body(*refs):
    out = refs[6]
    for p in range(2):
        a, b, c = refs[3 * p : 3 * p + 3]
        total = add3(a[...], b[...], c[...])
        for z in range(8):
            out[z, 64 * p : 64 * p + 64] = total[z * 64 : z * 64 + 64]
        for z in range(4):
            out[4 * p + z, 128:176] = total[512 + z * 48 : 560 + z * 48]


def sum_body(got, out):
    total = got[0].astype(F32)
    for k in range(1, 8):
        total += got[k].astype(F32)
    share = total.astype(BF)
    for k in range(8):
        out[k] = share


def unpack_body(got, stem, up, down):
    for y in range(4):
        for xl in range(2):
            piece = got[y * 2 + xl].astype(F32)
            col = (xl * 4 + y) * LANES
            down[:, col : col + LANES] = piece[0:64]
            stem[:, col : col + LANES] = piece[128:176]
            col = (y * 2 + xl) * 256
            up[:, col : col + LANES] = piece[64:96]
            up[:, col + LANES : col + 256] = piece[96:128]


def finish(pieces):
    share = [((8, ROWS, LANES), BF)]
    (packed,) = call(pack_body, share, [], "z_pack", *pieces, specs=[VMEM] * 6)
    got = lax.all_to_all(packed, "z", 0, 0, tiled=True)
    (copies,) = call(sum_body, share, [], "z_sum", got, specs=[VMEM])
    every = lax.all_to_all(copies, ("y", "xl"), 0, 0, tiled=True)
    outs = [((48, 1024), F32), ((32, 2048), F32), ((64, 1024), F32)]
    return call(unpack_body, outs, [], "unpack", every, specs=[VMEM])


def local(patches, stem_weight, ln_gain, up_weight, down_weight, cotangent):
    x = lax.axis_index("xh") * 2 + lax.axis_index("xl")
    pos = jnp.stack([x, lax.axis_index("y"), lax.axis_index("z"), lax.axis_index("c")])
    pos = pos.astype(jnp.int32)

    cot_other = move(cotangent, "c", 0)
    deriv, normal, inverse, mine, send = forward_pass(
        pos, ln_gain, patches, stem_weight, up_weight
    )
    other = move(send, "c", 0)

    over_cols = (((1,), (1,)), ((), ()))
    hidden_grad = lax.dot_general(cotangent, down_weight, over_cols, preferred_element_type=F32)
    preact_grad = (hidden_grad * deriv).astype(BF)
    preact_other = move(preact_grad, "c", 0)

    normal_grad = (
        lax.dot_general(preact_grad, up_weight, over_cols, preferred_element_type=F32) * ln_gain
    )
    first_mean = jnp.mean(normal_grad, axis=1, keepdims=True)
    second_mean = jnp.mean(normal_grad * normal, axis=1, keepdims=True)
    embed_grad = (
        cotangent.astype(F32) + inverse * (normal_grad - first_mean - normal * second_mean)
    ).astype(BF)
    embed_other = move(embed_grad, "c", 0)

    parts = terms(
        pos, (mine, other), (cotangent, cot_other), (preact_grad, preact_other), (embed_grad, embed_other)
    )
    return tuple(finish(reduce_xy(pos, parts)))


def solution(mesh):
    fine = Mesh(mesh.devices.reshape(4, 2, 8, 2, 2), AXES)
    rows = P(("z", "xh", "c"), None)
    in_specs = (P(AXES, None), P(), P(), P(), P(), P(AXES, None))
    return jax.shard_map(
        local, mesh=fine, in_specs=in_specs, out_specs=(rows, rows, rows), check_vma=False
    )
```

```python
import functools
import math

import jax
import jax.numpy as jnp
from jax import lax
from jax.experimental import pallas as pl
from jax.experimental.pallas import tpu as pltpu
from jax.sharding import Mesh, PartitionSpec as P

BF = jnp.bfloat16
F32 = jnp.float32
AXES = ("y", "xl", "z", "xh", "c")
VMEM = pl.BlockSpec(memory_space=pltpu.VMEM)
SMEM = pl.BlockSpec(memory_space=pltpu.SMEM)
LANES = 128
OVER_COLUMNS = (((1,), (1,)), ((), ()))


def move(value, axis, hop):
    pairs = []
    for y in range(4):
        for x in range(4):
            for z in range(8):
                for c in range(2):
                    far = hop * (1 - 2 * c)
                    X = (x + far) % 4 if axis == "x" else x
                    Y = (y + far) % 4 if axis == "y" else y
                    C = 1 - c if axis == "c" else c
                    src = (y * 2 + x % 2) * 32 + z * 4 + (x // 2) * 2 + c
                    dst = (Y * 2 + X % 2) * 32 + z * 4 + (X // 2) * 2 + C
                    pairs.append((src, dst))
    return lax.ppermute(value, AXES, sorted(pairs))


def call(body, outs, scratch, name, *operands, limit=8, specs=None, gflop=0.02):
    return pl.pallas_call(
        body,
        out_shape=[jax.ShapeDtypeStruct(s, d) for s, d in outs],
        in_specs=specs or [SMEM] + [VMEM] * (len(operands) - 1),
        out_specs=[VMEM] * len(outs),
        scratch_shapes=scratch,
        name=name,
        cost_estimate=pl.CostEstimate(
            flops=int(gflop * 1e9), bytes_accessed=1 << 20, transcendentals=0
        ),
        compiler_params=pltpu.CompilerParams(vmem_limit_bytes=limit << 20),
    )(*operands)


SHARE = 144


def gelu_pass_body(
    pos, gain_any, patches_any, cot_any, stem_any, up_any, down_any,
    preact_grad, normal, inverse, mine, send,
    p, g, w, u, d, gain, t, sem,
):
    plan = [(patches_any, p), (cot_any, g)]
    for k in range(3):
        rows = pl.ds(k * 512, 512)
        plan.append((stem_any.at[rows], w.at[rows]))
    for k in range(2):
        cols = pl.ds(k * 1024, 1024)
        plan.append((up_any.at[:, cols], u.at[:, cols]))
        plan.append((down_any.at[cols], d.at[cols]))
    plan.append((gain_any, gain))
    order = [0, 2, 3, 4, 9, 5, 1, 6, 7, 8]
    copies = [pltpu.make_async_copy(src, dst, sem.at[k]) for k, (src, dst) in enumerate(plan)]
    for k in order:
        copies[k].start()

    copies[0].wait()
    acc = None
    for k in range(3):
        copies[2 + k].wait()
        part = jnp.dot(
            p[:, k * 512 : k * 512 + 512], w[k * 512 : k * 512 + 512], preferred_element_type=F32
        )
        acc = part if acc is None else acc + part
    copies[9].wait()
    embed = acc.astype(BF).astype(F32)
    center = jnp.mean(embed, axis=1, keepdims=True)
    shifted = embed - center
    scale = lax.rsqrt(jnp.mean(shifted * shifted, axis=1, keepdims=True) + 1e-06)
    norm = shifted * scale
    normal[...] = norm
    inverse[...] = scale
    normed = (norm * gain[...]).astype(BF)
    pt = p[...].T
    nt = normed.T
    for b in range(16):
        for half in range(2):
            at = b * 2 + half
            t[b, half, 64:96] = nt[at * 32 : at * 32 + 32]
            t[b, half, 96:144] = pt[at * 48 : at * 48 + 48]
    copies[1].wait()
    for j in range(8):
        if j % 4 == 0:
            copies[5 + j // 2].wait()
            copies[6 + j // 2].wait()
        cols = slice(j * 256, j * 256 + 256)
        pre = jnp.dot(normed, u[:, cols], preferred_element_type=F32)
        grad = lax.dot_general(g[...], d[cols], OVER_COLUMNS, preferred_element_type=F32)
        cdf = 0.5 * (1.0 + lax.erf(pre * math.sqrt(0.5)))
        slope = cdf + pre * jnp.exp(-0.5 * pre * pre) * (1.0 / math.sqrt(2.0 * math.pi))
        preact_grad[:, cols] = (grad * slope).astype(BF)
        ht = (pre * cdf).astype(BF).T
        for q in range(4):
            t[j * 2 + q // 2, q % 2, 0:64] = ht[q * 64 : q * 64 + 64]
    c = pos[3]
    mine[...] = t[:, c]
    send[...] = t[:, 1 - c]


def gelu_pass(pos, gain, patches, cotangent, stem_weight, up_weight, down_weight):
    outs = [((256, 2048), BF), ((256, 1024), F32), ((256, 1), F32)]
    return call(
        gelu_pass_body,
        outs + [((16, SHARE, 256), BF)] * 2,
        [
            pltpu.VMEM((256, 1536), BF),
            pltpu.VMEM((256, 1024), BF),
            pltpu.VMEM((1536, 1024), BF),
            pltpu.VMEM((1024, 2048), BF),
            pltpu.VMEM((2048, 1024), BF),
            pltpu.VMEM((1, 1024), F32),
            pltpu.VMEM((16, 2, SHARE, 256), BF),
            pltpu.SemaphoreType.DMA((10,)),
        ],
        "gelu_pass",
        pos,
        gain,
        patches,
        cotangent,
        stem_weight,
        up_weight,
        down_weight,
        limit=48,
        specs=[SMEM] + [pl.BlockSpec(memory_space=pl.ANY)] * 6,
        gflop=8,
    )


def norm_back_body(gain, preact_grad, up, cot, normal, inverse, embed_grad):
    grad = lax.dot_general(preact_grad[...], up[...], OVER_COLUMNS, preferred_element_type=F32)
    grad = grad * gain[...]
    norm = normal[...]
    first = jnp.mean(grad, axis=1, keepdims=True)
    second = jnp.mean(grad * norm, axis=1, keepdims=True)
    embed_grad[...] = (
        cot[...].astype(F32) + inverse[...] * (grad - first - norm * second)
    ).astype(BF)


ROWS = 176
CHUNK = 704


def chunk_of(me, pos, rel):
    return lax.rem(me + rel * (1 + 2 * pos[3]), 4)


def dot2(lefts, rights):
    acc = jnp.dot(lefts[0], rights[0], preferred_element_type=F32)
    acc += jnp.dot(lefts[1], rights[1], preferred_element_type=F32)
    return acc.astype(BF)


def columns(ref, starts, width):
    parts = [ref[:, pl.ds(pl.multiple_of(start, LANES), width)] for start in starts]
    return parts[0] if len(parts) == 1 else jnp.concatenate(parts, axis=1)


def terms_x_body(pos, lm, lr, cm, cr, gm, gr, *outs):
    for rel in range(4):
        to = chunk_of(pos[0], pos, rel)
        xh, xl = to // 2, lax.rem(to, 2)
        dst = outs[rel]
        acc = dot2(
            [ref[:, xh, 0:64].reshape(512, 256) for ref in (lm, lr)],
            [columns(ref, [xl * 512], 512) for ref in (cm, cr)],
        )
        for yy in range(4):
            dst[yy, 0:512] = acc[:, yy * 128 : yy * 128 + 128]
        acc = dot2(
            [ref[0:3, xh, 64:96].reshape(96, 256) for ref in (lm, lr)],
            [columns(ref, [(yy * 2 + xl) * 256 for yy in range(4)], 256) for ref in (gm, gr)],
        )
        for z in range(3):
            for yy in range(4):
                for k in range(2):
                    at, col = 512 + z * 64 + k * 32, (yy * 2 + k) * 128
                    dst[yy, at : at + 32] = acc[z * 32 : z * 32 + 32, col : col + 128]


def terms_y_body(pos, lm, lr, gm, gr, em, er, *outs):
    for rel in range(4):
        to = chunk_of(pos[1], pos, rel)
        dst = outs[rel]
        acc = dot2(
            [ref[3:8, :, 64:96].reshape(320, 256) for ref in (lm, lr)],
            [columns(ref, [to * 512], 512) for ref in (gm, gr)],
        )
        for z in range(5):
            for xx in range(4):
                for k in range(2):
                    row, col = (z * 2 + xx // 2) * 32, (xx % 2 * 2 + k) * 128
                    at = z * 64 + k * 32
                    dst[xx, at : at + 32] = acc[row : row + 32, col : col + 128]
        acc = dot2(
            [ref[:, :, 96:144].reshape(768, 256) for ref in (lm, lr)],
            [columns(ref, [to * 128, 512 + to * 128], 128) for ref in (em, er)],
        )
        for z in range(8):
            for xx in range(4):
                row, col = (z * 2 + xx // 2) * 48, xx % 2 * 128
                at = 320 + z * 48
                dst[xx, at : at + 48] = acc[row : row + 48, col : col + 128]


def pass_on_body(keep, got, out):
    out[...] = (keep[...].astype(F32) + got[...].astype(F32)).astype(BF)


def rings(axes, parts):
    result = []
    for axis, (own, keep, ahead, behind) in zip(axes, parts):
        got = move(ahead, axis, 1)
        near = move(behind, axis, -1)
        (total,) = call(
            pass_on_body, [(keep.shape, BF)], [], "pass_on", keep, got, specs=[VMEM, VMEM]
        )
        result += [own, near, move(total, axis, 1)]
    return result


def add3(a, b, c):
    return (a.astype(F32) + b.astype(F32) + c.astype(F32)).astype(BF)


def turn_body(pos, *refs):
    for p in range(2):
        a, b, c = refs[3 * p : 3 * p + 3]
        for rel in range(4):
            to = chunk_of(pos[1 - p], pos, rel)
            refs[6 + 4 * p + rel][...] = add3(a[to], b[to], c[to])


def reduce_xy(pos, parts):
    outs = call(
        turn_body, [((CHUNK, LANES), BF)] * 8, [], "ring_turn", pos, *rings("xy", parts)
    )
    return rings("yx", (outs[:4], outs[4:]))


def pack_body(*refs):
    out = refs[6]
    x, y = (add3(*(ref[...] for ref in refs[3 * p : 3 * p + 3])) for p in range(2))
    for z in range(8):
        out[z, 0:64] = x[z * 64 : z * 64 + 64]
        out[z, 64:128] = x[512 + z * 64 : 576 + z * 64] if z < 3 else y[z * 64 - 192 : z * 64 - 128]
        out[z, 128:176] = y[320 + z * 48 : 368 + z * 48]


def sum_body(got, out):
    total = got[0].astype(F32)
    for k in range(1, 8):
        total += got[k].astype(F32)
    share = total.astype(BF)
    for k in range(8):
        out[k] = share


def unpack_body(got, stem, up, down):
    for y in range(4):
        for xl in range(2):
            piece = got[y * 2 + xl].astype(F32)
            col = (xl * 4 + y) * LANES
            down[:, col : col + LANES] = piece[0:64]
            stem[:, col : col + LANES] = piece[128:176]
            col = (y * 2 + xl) * 256
            up[:, col : col + LANES] = piece[64:96]
            up[:, col + LANES : col + 256] = piece[96:128]


def finish(pieces):
    share = [((8, ROWS, LANES), BF)]
    (packed,) = call(pack_body, share, [], "z_pack", *pieces, specs=[VMEM] * 6)
    got = lax.all_to_all(packed, "z", 0, 0, tiled=True)
    (copies,) = call(sum_body, share, [], "z_sum", got, specs=[VMEM])
    every = lax.all_to_all(copies, ("y", "xl"), 0, 0, tiled=True)
    outs = [((48, 1024), F32), ((32, 2048), F32), ((64, 1024), F32)]
    return call(unpack_body, outs, [], "unpack", every, specs=[VMEM])


def local(patches, stem_weight, ln_gain, up_weight, down_weight, cotangent):
    x = lax.axis_index("xh") * 2 + lax.axis_index("xl")
    pos = jnp.stack([x, lax.axis_index("y"), lax.axis_index("z"), lax.axis_index("c")])
    pos = pos.astype(jnp.int32)

    gain = ln_gain.reshape(1, 1024)
    cot_other = move(cotangent, "c", 0)
    preact_grad, normal, inverse, mine, send = gelu_pass(
        pos, gain, patches, cotangent, stem_weight, up_weight, down_weight
    )
    other = move(send, "c", 0)
    preact_other = move(preact_grad, "c", 0)
    (embed_grad,) = call(
        norm_back_body,
        [((256, 1024), BF)],
        [],
        "norm_back",
        gain,
        preact_grad,
        up_weight,
        cotangent,
        normal,
        inverse,
        specs=[VMEM] * 6,
        limit=16,
        gflop=2,
    )
    embed_other = move(embed_grad, "c", 0)

    left = [v.reshape(8, 2, SHARE, 256) for v in (mine, other)]
    outs = [((4, CHUNK, LANES), BF)] * 4
    grads = (preact_grad, preact_other)
    part_x = call(
        terms_x_body, outs, [], "terms_x", pos, *left, cotangent, cot_other, *grads, limit=16, gflop=2
    )
    embed_other, *part_x = lax.optimization_barrier((embed_other, *part_x))
    part_y = call(
        terms_y_body, outs, [], "terms_y", pos, *left, *grads, embed_grad, embed_other, limit=16, gflop=2
    )
    return tuple(finish(reduce_xy(pos, (part_x, part_y))))


def solution(mesh):
    fine = Mesh(mesh.devices.reshape(4, 2, 8, 2, 2), AXES)
    rows = P(("z", "xh", "c"), None)
    in_specs = (P(AXES, None), P(), P(), P(), P(), P(AXES, None))
    return jax.shard_map(
        local, mesh=fine, in_specs=in_specs, out_specs=(rows, rows, rows), check_vma=False
    )
```

```python
import functools
import math

import jax
import jax.numpy as jnp
from jax import lax
from jax.experimental import pallas as pl
from jax.experimental.pallas import tpu as pltpu
from jax.sharding import Mesh, PartitionSpec as P

BF = jnp.bfloat16
F32 = jnp.float32
AXES = ("y", "xl", "z", "xh", "c")
VMEM = pl.BlockSpec(memory_space=pltpu.VMEM)
SMEM = pl.BlockSpec(memory_space=pltpu.SMEM)
LANES = 128
OVER_COLUMNS = (((1,), (1,)), ((), ()))


def move(value, axis, hop):
    pairs = []
    for y in range(4):
        for x in range(4):
            for z in range(8):
                for c in range(2):
                    far = hop * (1 - 2 * c)
                    X = (x + far) % 4 if axis == "x" else x
                    Y = (y + far) % 4 if axis == "y" else y
                    C = 1 - c if axis == "c" else c
                    src = (y * 2 + x % 2) * 32 + z * 4 + (x // 2) * 2 + c
                    dst = (Y * 2 + X % 2) * 32 + z * 4 + (X // 2) * 2 + C
                    pairs.append((src, dst))
    return lax.ppermute(value, AXES, sorted(pairs))


def call(body, outs, scratch, name, *operands, limit=8, specs=None, gflop=0.02):
    return pl.pallas_call(
        body,
        out_shape=[jax.ShapeDtypeStruct(s, d) for s, d in outs],
        in_specs=specs or [SMEM] + [VMEM] * (len(operands) - 1),
        out_specs=[VMEM] * len(outs),
        scratch_shapes=scratch,
        name=name,
        cost_estimate=pl.CostEstimate(
            flops=int(gflop * 1e9), bytes_accessed=1 << 20, transcendentals=0
        ),
        compiler_params=pltpu.CompilerParams(vmem_limit_bytes=limit << 20),
    )(*operands)


SHARE = 144


def gelu_pass_body(
    pos, gain, p, g, stem_any, up_any, down_any,
    preact_grad, normal, inverse, mine, send,
    w, u, d, t, sem,
):
    plan = []
    for k in range(3):
        rows = pl.ds(k * 512, 512)
        plan.append((stem_any.at[rows], w.at[rows]))
    for k in range(2):
        cols = pl.ds(k * 1024, 1024)
        plan.append((up_any.at[:, cols], u.at[:, cols]))
        plan.append((down_any.at[cols], d.at[cols]))
    copies = [pltpu.make_async_copy(src, dst, sem.at[k]) for k, (src, dst) in enumerate(plan)]
    for copy in copies:
        copy.start()

    pt = p[...].T
    for b in range(16):
        for half in range(2):
            at = (b * 2 + half) * 48
            t[b, half, 96:144] = pt[at : at + 48]
    acc = None
    for k in range(3):
        copies[k].wait()
        part = jnp.dot(
            p[:, k * 512 : k * 512 + 512], w[k * 512 : k * 512 + 512], preferred_element_type=F32
        )
        acc = part if acc is None else acc + part
    embed = acc.astype(BF).astype(F32)
    center = jnp.mean(embed, axis=1, keepdims=True)
    shifted = embed - center
    scale = lax.rsqrt(jnp.mean(shifted * shifted, axis=1, keepdims=True) + 1e-06)
    norm = shifted * scale
    normal[...] = norm
    inverse[...] = scale
    normed = (norm * gain[...]).astype(BF)
    nt = normed.T
    for b in range(16):
        for half in range(2):
            at = b * 2 + half
            t[b, half, 64:96] = nt[at * 32 : at * 32 + 32]
    for j in range(8):
        if j % 4 == 0:
            copies[3 + j // 2].wait()
            copies[4 + j // 2].wait()
        cols = slice(j * 256, j * 256 + 256)
        pre = jnp.dot(normed, u[:, cols], preferred_element_type=F32)
        grad = lax.dot_general(g[...], d[cols], OVER_COLUMNS, preferred_element_type=F32)
        cdf = 0.5 * (1.0 + lax.erf(pre * math.sqrt(0.5)))
        slope = cdf + pre * jnp.exp(-0.5 * pre * pre) * (1.0 / math.sqrt(2.0 * math.pi))
        preact_grad[:, cols] = (grad * slope).astype(BF)
        ht = (pre * cdf).astype(BF).T
        for q in range(4):
            t[j * 2 + q // 2, q % 2, 0:64] = ht[q * 64 : q * 64 + 64]
    c = pos[3]
    mine[...] = t[:, c]
    send[...] = t[:, 1 - c]


def gelu_pass(pos, gain, patches, cotangent, stem_weight, up_weight, down_weight):
    outs = [((256, 2048), BF), ((256, 1024), F32), ((256, 1), F32)]
    return call(
        gelu_pass_body,
        outs + [((16, SHARE, 256), BF)] * 2,
        [
            pltpu.VMEM((1536, 1024), BF),
            pltpu.VMEM((1024, 2048), BF),
            pltpu.VMEM((2048, 1024), BF),
            pltpu.VMEM((16, 2, SHARE, 256), BF),
            pltpu.SemaphoreType.DMA((7,)),
        ],
        "gelu_pass",
        pos,
        gain,
        patches,
        cotangent,
        stem_weight,
        up_weight,
        down_weight,
        limit=48,
        specs=[SMEM] + [VMEM] * 3 + [pl.BlockSpec(memory_space=pl.ANY)] * 3,
        gflop=8,
    )


def norm_back_body(gain, preact_grad, up, cot, normal, inverse, embed_grad):
    grad = lax.dot_general(preact_grad[...], up[...], OVER_COLUMNS, preferred_element_type=F32)
    grad = grad * gain[...]
    norm = normal[...]
    first = jnp.mean(grad, axis=1, keepdims=True)
    second = jnp.mean(grad * norm, axis=1, keepdims=True)
    embed_grad[...] = (
        cot[...].astype(F32) + inverse[...] * (grad - first - norm * second)
    ).astype(BF)


ROWS = 176
SPLIT = 4
CHUNK_X = 512 + SPLIT * 64
CHUNK_Y = (8 - SPLIT) * 64 + 384


def chunk_of(me, pos, rel):
    return lax.rem(me + rel * (1 + 2 * pos[3]), 4)


def dot2(lefts, rights):
    acc = jnp.dot(lefts[0], rights[0], preferred_element_type=F32)
    acc += jnp.dot(lefts[1], rights[1], preferred_element_type=F32)
    return acc.astype(BF)


def columns(ref, starts, width):
    parts = [ref[:, pl.ds(pl.multiple_of(start, LANES), width)] for start in starts]
    return parts[0] if len(parts) == 1 else jnp.concatenate(parts, axis=1)


def terms_x_body(pos, lm, lr, cm, cr, gm, gr, *outs):
    for rel in range(4):
        to = chunk_of(pos[0], pos, rel)
        xh, xl = to // 2, lax.rem(to, 2)
        dst = outs[rel]
        acc = dot2(
            [ref[:, xh, 0:64].reshape(512, 256) for ref in (lm, lr)],
            [columns(ref, [xl * 512], 512) for ref in (cm, cr)],
        )
        for yy in range(4):
            dst[yy, 0:512] = acc[:, yy * 128 : yy * 128 + 128]
        acc = dot2(
            [ref[0:SPLIT, xh, 64:96].reshape(SPLIT * 32, 256) for ref in (lm, lr)],
            [columns(ref, [(yy * 2 + xl) * 256 for yy in range(4)], 256) for ref in (gm, gr)],
        )
        for z in range(SPLIT):
            for yy in range(4):
                for k in range(2):
                    at, col = 512 + z * 64 + k * 32, (yy * 2 + k) * 128
                    dst[yy, at : at + 32] = acc[z * 32 : z * 32 + 32, col : col + 128]


def terms_y_body(pos, lm, lr, gm, gr, em, er, *outs):
    for rel in range(4):
        to = chunk_of(pos[1], pos, rel)
        dst = outs[rel]
        acc = dot2(
            [ref[SPLIT:8, :, 64:96].reshape((8 - SPLIT) * 64, 256) for ref in (lm, lr)],
            [columns(ref, [to * 512], 512) for ref in (gm, gr)],
        )
        for z in range(8 - SPLIT):
            for xx in range(4):
                for k in range(2):
                    row, col = (z * 2 + xx // 2) * 32, (xx % 2 * 2 + k) * 128
                    at = z * 64 + k * 32
                    dst[xx, at : at + 32] = acc[row : row + 32, col : col + 128]
        acc = dot2(
            [ref[:, :, 96:144].reshape(768, 256) for ref in (lm, lr)],
            [columns(ref, [to * 128, 512 + to * 128], 128) for ref in (em, er)],
        )
        for z in range(8):
            for xx in range(4):
                row, col = (z * 2 + xx // 2) * 48, xx % 2 * 128
                at = CHUNK_Y - 384 + z * 48
                dst[xx, at : at + 48] = acc[row : row + 48, col : col + 128]


def pass_on_body(keep, got, out):
    out[...] = (keep[...].astype(F32) + got[...].astype(F32)).astype(BF)


def rings(axes, parts):
    result = []
    for axis, (own, keep, ahead, behind) in zip(axes, parts):
        got = move(ahead, axis, 1)
        near = move(behind, axis, -1)
        (total,) = call(
            pass_on_body, [(keep.shape, BF)], [], "pass_on", keep, got, specs=[VMEM, VMEM]
        )
        result += [own, near, move(total, axis, 1)]
    return result


def add3(a, b, c):
    return (a.astype(F32) + b.astype(F32) + c.astype(F32)).astype(BF)


def turn_body(pos, *refs):
    for p in range(2):
        a, b, c = refs[3 * p : 3 * p + 3]
        for rel in range(4):
            to = chunk_of(pos[1 - p], pos, rel)
            refs[6 + 4 * p + rel][...] = add3(a[to], b[to], c[to])


def reduce_xy(pos, parts):
    outs = [((CHUNK_X, LANES), BF)] * 4 + [((CHUNK_Y, LANES), BF)] * 4
    outs = call(turn_body, outs, [], "ring_turn", pos, *rings("xy", parts))
    return rings("yx", (outs[:4], outs[4:]))


def pack_body(*refs):
    out = refs[6]
    x, y = (add3(*(ref[...] for ref in refs[3 * p : 3 * p + 3])) for p in range(2))
    for z in range(8):
        out[z, 0:64] = x[z * 64 : z * 64 + 64]
        up, at = (x, 512 + z * 64) if z < SPLIT else (y, (z - SPLIT) * 64)
        out[z, 64:128] = up[at : at + 64]
        at = CHUNK_Y - 384 + z * 48
        out[z, 128:176] = y[at : at + 48]


def sum_body(got, out):
    total = got[0].astype(F32)
    for k in range(1, 8):
        total += got[k].astype(F32)
    share = total.astype(BF)
    for k in range(8):
        out[k] = share


def unpack_body(got, stem, up, down):
    for y in range(4):
        for xl in range(2):
            piece = got[y * 2 + xl].astype(F32)
            col = (xl * 4 + y) * LANES
            down[:, col : col + LANES] = piece[0:64]
            stem[:, col : col + LANES] = piece[128:176]
            col = (y * 2 + xl) * 256
            up[:, col : col + LANES] = piece[64:96]
            up[:, col + LANES : col + 256] = piece[96:128]


def finish(pieces):
    share = [((8, ROWS, LANES), BF)]
    (packed,) = call(pack_body, share, [], "z_pack", *pieces, specs=[VMEM] * 6)
    got = lax.all_to_all(packed, "z", 0, 0, tiled=True)
    (copies,) = call(sum_body, share, [], "z_sum", got, specs=[VMEM])
    every = lax.all_to_all(copies, ("y", "xl"), 0, 0, tiled=True)
    outs = [((48, 1024), F32), ((32, 2048), F32), ((64, 1024), F32)]
    return call(unpack_body, outs, [], "unpack", every, specs=[VMEM])


def local(patches, stem_weight, ln_gain, up_weight, down_weight, cotangent):
    x = lax.axis_index("xh") * 2 + lax.axis_index("xl")
    pos = jnp.stack([x, lax.axis_index("y"), lax.axis_index("z"), lax.axis_index("c")])
    pos = pos.astype(jnp.int32)

    gain = ln_gain.reshape(1, 1024)
    cot_other = move(cotangent, "c", 0)
    preact_grad, normal, inverse, mine, send = gelu_pass(
        pos, gain, patches, cotangent, stem_weight, up_weight, down_weight
    )
    other = move(send, "c", 0)
    preact_other = move(preact_grad, "c", 0)
    (embed_grad,) = call(
        norm_back_body,
        [((256, 1024), BF)],
        [],
        "norm_back",
        gain,
        preact_grad,
        up_weight,
        cotangent,
        normal,
        inverse,
        specs=[VMEM] * 6,
        limit=16,
        gflop=2,
    )
    embed_other = move(embed_grad, "c", 0)

    left = [v.reshape(8, 2, SHARE, 256) for v in (mine, other)]
    outs_x, outs_y = ([((4, rows, LANES), BF)] * 4 for rows in (CHUNK_X, CHUNK_Y))
    grads = (preact_grad, preact_other)
    part_x = call(
        terms_x_body, outs_x, [], "terms_x", pos, *left, cotangent, cot_other, *grads, limit=16, gflop=2
    )
    embed_other, *part_x = lax.optimization_barrier((embed_other, *part_x))
    part_y = call(
        terms_y_body, outs_y, [], "terms_y", pos, *left, *grads, embed_grad, embed_other, limit=16, gflop=2
    )
    return tuple(finish(reduce_xy(pos, (part_x, part_y))))


def solution(mesh):
    fine = Mesh(mesh.devices.reshape(4, 2, 8, 2, 2), AXES)
    rows = P(("z", "xh", "c"), None)
    in_specs = (P(AXES, None), P(), P(), P(), P(), P(AXES, None))
    return jax.shard_map(
        local, mesh=fine, in_specs=in_specs, out_specs=(rows, rows, rows), check_vma=False
    )
```

```python
import functools
import math

import jax
import jax.numpy as jnp
from jax import lax
from jax.experimental import pallas as pl
from jax.experimental.pallas import tpu as pltpu
from jax.sharding import Mesh, PartitionSpec as P

BF = jnp.bfloat16
F32 = jnp.float32
AXES = ("y", "xl", "z", "xh", "c")
VMEM = pl.BlockSpec(memory_space=pltpu.VMEM)
SMEM = pl.BlockSpec(memory_space=pltpu.SMEM)
LANES = 128
OVER_COLUMNS = (((1,), (1,)), ((), ()))


def move(value, axis, hop):
    pairs = []
    for y in range(4):
        for x in range(4):
            for z in range(8):
                for c in range(2):
                    far = hop * (1 - 2 * c)
                    X = (x + far) % 4 if axis == "x" else x
                    Y = (y + far) % 4 if axis == "y" else y
                    C = 1 - c if axis == "c" else c
                    src = (y * 2 + x % 2) * 32 + z * 4 + (x // 2) * 2 + c
                    dst = (Y * 2 + X % 2) * 32 + z * 4 + (X // 2) * 2 + C
                    pairs.append((src, dst))
    return lax.ppermute(value, AXES, sorted(pairs))


def call(body, outs, scratch, name, *operands, limit=8, specs=None, gflop=0.02):
    return pl.pallas_call(
        body,
        out_shape=[jax.ShapeDtypeStruct(s, d) for s, d in outs],
        in_specs=specs or [SMEM] + [VMEM] * (len(operands) - 1),
        out_specs=[VMEM] * len(outs),
        scratch_shapes=scratch,
        name=name,
        cost_estimate=pl.CostEstimate(
            flops=int(gflop * 1e9), bytes_accessed=1 << 20, transcendentals=0
        ),
        compiler_params=pltpu.CompilerParams(vmem_limit_bytes=limit << 20),
    )(*operands)


SHARE = 144


def gelu_pass_body(
    pos, gain, p, g, stem_any, up_any, down_any,
    preact_grad, normal, inverse, mine, send,
    w, u, d, t, sem,
):
    plan = []
    for k in range(3):
        rows = pl.ds(k * 512, 512)
        plan.append((stem_any.at[rows], w.at[rows]))
    for k in range(2):
        cols = pl.ds(k * 1024, 1024)
        plan.append((up_any.at[:, cols], u.at[:, cols]))
        plan.append((down_any.at[cols], d.at[cols]))
    copies = [pltpu.make_async_copy(src, dst, sem.at[k]) for k, (src, dst) in enumerate(plan)]
    for copy in copies:
        copy.start()

    pt = p[...].T
    for b in range(16):
        for half in range(2):
            at = (b * 2 + half) * 48
            t[b, half, 96:144] = pt[at : at + 48]
    acc = None
    for k in range(3):
        copies[k].wait()
        part = jnp.dot(
            p[:, k * 512 : k * 512 + 512], w[k * 512 : k * 512 + 512], preferred_element_type=F32
        )
        acc = part if acc is None else acc + part
    embed = acc.astype(BF).astype(F32)
    center = jnp.mean(embed, axis=1, keepdims=True)
    shifted = embed - center
    scale = lax.rsqrt(jnp.mean(shifted * shifted, axis=1, keepdims=True) + 1e-06)
    norm = shifted * scale
    normal[...] = norm
    inverse[...] = scale
    normed = (norm * gain[...]).astype(BF)
    nt = normed.T
    for b in range(16):
        for half in range(2):
            at = b * 2 + half
            t[b, half, 64:96] = nt[at * 32 : at * 32 + 32]
    for j in range(8):
        if j % 4 == 0:
            copies[3 + j // 2].wait()
            copies[4 + j // 2].wait()
        cols = slice(j * 256, j * 256 + 256)
        pre = jnp.dot(normed, u[:, cols], preferred_element_type=F32)
        grad = lax.dot_general(g[...], d[cols], OVER_COLUMNS, preferred_element_type=F32)
        cdf = 0.5 * (1.0 + lax.erf(pre * math.sqrt(0.5)))
        slope = cdf + pre * jnp.exp(-0.5 * pre * pre) * (1.0 / math.sqrt(2.0 * math.pi))
        preact_grad[:, cols] = (grad * slope).astype(BF)
        ht = (pre * cdf).astype(BF).T
        for q in range(4):
            t[j * 2 + q // 2, q % 2, 0:64] = ht[q * 64 : q * 64 + 64]
    c = pos[3]
    mine[...] = t[:, c]
    send[...] = t[:, 1 - c]


def gelu_pass(pos, gain, patches, cotangent, stem_weight, up_weight, down_weight):
    outs = [((256, 2048), BF), ((256, 1024), F32), ((256, 1), F32)]
    return call(
        gelu_pass_body,
        outs + [((16, SHARE, 256), BF)] * 2,
        [
            pltpu.VMEM((1536, 1024), BF),
            pltpu.VMEM((1024, 2048), BF),
            pltpu.VMEM((2048, 1024), BF),
            pltpu.VMEM((16, 2, SHARE, 256), BF),
            pltpu.SemaphoreType.DMA((7,)),
        ],
        "gelu_pass",
        pos,
        gain,
        patches,
        cotangent,
        stem_weight,
        up_weight,
        down_weight,
        limit=48,
        specs=[SMEM] + [VMEM] * 3 + [pl.BlockSpec(memory_space=pl.ANY)] * 3,
        gflop=8,
    )


def norm_back_body(gain, preact_grad, up, cot, normal, inverse, embed_grad):
    grad = lax.dot_general(preact_grad[...], up[...], OVER_COLUMNS, preferred_element_type=F32)
    grad = grad * gain[...]
    norm = normal[...]
    first = jnp.mean(grad, axis=1, keepdims=True)
    second = jnp.mean(grad * norm, axis=1, keepdims=True)
    embed_grad[...] = (
        cot[...].astype(F32) + inverse[...] * (grad - first - norm * second)
    ).astype(BF)


ROWS = 176
SPLIT = 4
CHUNK_X = 512 + SPLIT * 64
CHUNK_Y = (8 - SPLIT) * 64 + 384


def chunk_of(me, pos, rel):
    return lax.rem(me + rel * (1 + 2 * pos[3]), 4)


def dot2(lefts, rights):
    acc = jnp.dot(lefts[0], rights[0], preferred_element_type=F32)
    acc += jnp.dot(lefts[1], rights[1], preferred_element_type=F32)
    return acc.astype(BF)


def columns(ref, starts, width):
    parts = [ref[:, pl.ds(pl.multiple_of(start, LANES), width)] for start in starts]
    return parts[0] if len(parts) == 1 else jnp.concatenate(parts, axis=1)


def terms_x_body(pos, lm, lr, cm, cr, gm, gr, *outs):
    for rel in range(4):
        to = chunk_of(pos[0], pos, rel)
        xh, xl = to // 2, lax.rem(to, 2)
        dst = outs[rel]
        acc = dot2(
            [ref[:, xh, 0:64].reshape(512, 256) for ref in (lm, lr)],
            [columns(ref, [xl * 512], 512) for ref in (cm, cr)],
        )
        for yy in range(4):
            dst[yy, 0:512] = acc[:, yy * 128 : yy * 128 + 128]
        acc = dot2(
            [ref[0:SPLIT, xh, 64:96].reshape(SPLIT * 32, 256) for ref in (lm, lr)],
            [columns(ref, [(yy * 2 + xl) * 256 for yy in range(4)], 256) for ref in (gm, gr)],
        )
        for z in range(SPLIT):
            for yy in range(4):
                for k in range(2):
                    at, col = 512 + z * 64 + k * 32, (yy * 2 + k) * 128
                    dst[yy, at : at + 32] = acc[z * 32 : z * 32 + 32, col : col + 128]


def terms_y_body(pos, lm, lr, gm, gr, em, er, *outs):
    for rel in range(4):
        to = chunk_of(pos[1], pos, rel)
        dst = outs[rel]
        acc = dot2(
            [ref[SPLIT:8, :, 64:96].reshape((8 - SPLIT) * 64, 256) for ref in (lm, lr)],
            [columns(ref, [to * 512], 512) for ref in (gm, gr)],
        )
        for z in range(8 - SPLIT):
            for xx in range(4):
                for k in range(2):
                    row, col = (z * 2 + xx // 2) * 32, (xx % 2 * 2 + k) * 128
                    at = z * 64 + k * 32
                    dst[xx, at : at + 32] = acc[row : row + 32, col : col + 128]
        acc = dot2(
            [ref[:, :, 96:144].reshape(768, 256) for ref in (lm, lr)],
            [columns(ref, [to * 128, 512 + to * 128], 128) for ref in (em, er)],
        )
        for z in range(8):
            for xx in range(4):
                row, col = (z * 2 + xx // 2) * 48, xx % 2 * 128
                at = CHUNK_Y - 384 + z * 48
                dst[xx, at : at + 48] = acc[row : row + 48, col : col + 128]


def pass_on_body(keep, got, out):
    out[...] = (keep[...].astype(F32) + got[...].astype(F32)).astype(BF)


def rings(axes, parts):
    result = []
    for p, (axis, (own, keep, ahead, behind)) in enumerate(zip(axes, parts)):
        got = move(ahead, axis, 1)
        near = move(behind, axis, -1)
        if p == 1:
            got, near = lax.optimization_barrier((got, near))
        (total,) = call(
            pass_on_body, [(keep.shape, BF)], [], "pass_on", keep, got, specs=[VMEM, VMEM]
        )
        result += [own, near, move(total, axis, 1)]
    return result


def add3(a, b, c):
    return (a.astype(F32) + b.astype(F32) + c.astype(F32)).astype(BF)


def turn_body(second, pos, own, near, far, *outs):
    for rel in range(4):
        to = chunk_of(pos[second], pos, rel)
        outs[rel][...] = add3(own[to], near[to], far[to])


def reduce_xy(pos, parts):
    sums = rings("xy", parts)
    turned = [
        call(
            functools.partial(turn_body, 1 - p),
            [(sums[3 * p].shape[1:], BF)] * 4,
            [],
            "ring_turn_" + "xy"[p],
            pos,
            *sums[3 * p : 3 * p + 3],
        )
        for p in range(2)
    ]
    return rings("yx", turned)


def pack_body(*refs):
    out = refs[6]
    x, y = (add3(*(ref[...] for ref in refs[3 * p : 3 * p + 3])) for p in range(2))
    for z in range(8):
        out[z, 0:64] = x[z * 64 : z * 64 + 64]
        up, at = (x, 512 + z * 64) if z < SPLIT else (y, (z - SPLIT) * 64)
        out[z, 64:128] = up[at : at + 64]
        at = CHUNK_Y - 384 + z * 48
        out[z, 128:176] = y[at : at + 48]


def sum_body(got, out):
    total = got[0].astype(F32)
    for k in range(1, 8):
        total += got[k].astype(F32)
    share = total.astype(BF)
    for k in range(8):
        out[k] = share


def unpack_body(got, stem, up, down):
    for y in range(4):
        for xl in range(2):
            piece = got[y * 2 + xl].astype(F32)
            col = (xl * 4 + y) * LANES
            down[:, col : col + LANES] = piece[0:64]
            stem[:, col : col + LANES] = piece[128:176]
            col = (y * 2 + xl) * 256
            up[:, col : col + LANES] = piece[64:96]
            up[:, col + LANES : col + 256] = piece[96:128]


def finish(pieces):
    share = [((8, ROWS, LANES), BF)]
    (packed,) = call(pack_body, share, [], "z_pack", *pieces, specs=[VMEM] * 6)
    got = lax.all_to_all(packed, "z", 0, 0, tiled=True)
    (copies,) = call(sum_body, share, [], "z_sum", got, specs=[VMEM])
    every = lax.all_to_all(copies, ("y", "xl"), 0, 0, tiled=True)
    outs = [((48, 1024), F32), ((32, 2048), F32), ((64, 1024), F32)]
    return call(unpack_body, outs, [], "unpack", every, specs=[VMEM])


def local(patches, stem_weight, ln_gain, up_weight, down_weight, cotangent):
    x = lax.axis_index("xh") * 2 + lax.axis_index("xl")
    pos = jnp.stack([x, lax.axis_index("y"), lax.axis_index("z"), lax.axis_index("c")])
    pos = pos.astype(jnp.int32)

    gain = ln_gain.reshape(1, 1024)
    cot_other = move(cotangent, "c", 0)
    preact_grad, normal, inverse, mine, send = gelu_pass(
        pos, gain, patches, cotangent, stem_weight, up_weight, down_weight
    )
    other = move(send, "c", 0)
    preact_other = move(preact_grad, "c", 0)
    (embed_grad,) = call(
        norm_back_body,
        [((256, 1024), BF)],
        [],
        "norm_back",
        gain,
        preact_grad,
        up_weight,
        cotangent,
        normal,
        inverse,
        specs=[VMEM] * 6,
        limit=16,
        gflop=2,
    )
    embed_other = move(embed_grad, "c", 0)

    left = [v.reshape(8, 2, SHARE, 256) for v in (mine, other)]
    outs_x, outs_y = ([((4, rows, LANES), BF)] * 4 for rows in (CHUNK_X, CHUNK_Y))
    grads = (preact_grad, preact_other)
    part_x = call(
        terms_x_body, outs_x, [], "terms_x", pos, *left, cotangent, cot_other, *grads, limit=16, gflop=2
    )
    embed_other, *part_x = lax.optimization_barrier((embed_other, *part_x))
    part_y = call(
        terms_y_body, outs_y, [], "terms_y", pos, *left, *grads, embed_grad, embed_other, limit=16, gflop=2
    )
    return tuple(finish(reduce_xy(pos, (part_x, part_y))))


def solution(mesh):
    fine = Mesh(mesh.devices.reshape(4, 2, 8, 2, 2), AXES)
    rows = P(("z", "xh", "c"), None)
    in_specs = (P(AXES, None), P(), P(), P(), P(), P(AXES, None))
    return jax.shard_map(
        local, mesh=fine, in_specs=in_specs, out_specs=(rows, rows, rows), check_vma=False
    )
```

```python
import functools
import math

import jax
import jax.numpy as jnp
from jax import lax
from jax.experimental import pallas as pl
from jax.experimental.pallas import tpu as pltpu
from jax.sharding import Mesh, PartitionSpec as P

BF = jnp.bfloat16
F32 = jnp.float32
AXES = ("y", "xl", "z", "xh", "c")
VMEM = pl.BlockSpec(memory_space=pltpu.VMEM)
SMEM = pl.BlockSpec(memory_space=pltpu.SMEM)
LANES = 128
OVER_COLUMNS = (((1,), (1,)), ((), ()))


def move(value, axis, hop):
    pairs = []
    for y in range(4):
        for x in range(4):
            for z in range(8):
                for c in range(2):
                    far = hop * (1 - 2 * c)
                    X = (x + far) % 4 if axis == "x" else x
                    Y = (y + far) % 4 if axis == "y" else y
                    C = 1 - c if axis == "c" else c
                    src = (y * 2 + x % 2) * 32 + z * 4 + (x // 2) * 2 + c
                    dst = (Y * 2 + X % 2) * 32 + z * 4 + (X // 2) * 2 + C
                    pairs.append((src, dst))
    return lax.ppermute(value, AXES, sorted(pairs))


def call(body, outs, scratch, name, *operands, limit=8, specs=None, gflop=0.02):
    return pl.pallas_call(
        body,
        out_shape=[jax.ShapeDtypeStruct(s, d) for s, d in outs],
        in_specs=specs or [SMEM] + [VMEM] * (len(operands) - 1),
        out_specs=[VMEM] * len(outs),
        scratch_shapes=scratch,
        name=name,
        cost_estimate=pl.CostEstimate(
            flops=int(gflop * 1e9), bytes_accessed=1 << 20, transcendentals=0
        ),
        compiler_params=pltpu.CompilerParams(vmem_limit_bytes=limit << 20),
    )(*operands)


SHARE = 144


def gelu_pass_body(
    pos, gain, p, g, stem_any, up_any, down_any,
    preact_grad, normal, inverse, mine, send,
    w, u, d, t, sem,
):
    plan = []
    for k in range(3):
        rows = pl.ds(k * 512, 512)
        plan.append((stem_any.at[rows], w.at[rows]))
    for k in range(2):
        cols = pl.ds(k * 1024, 1024)
        plan.append((up_any.at[:, cols], u.at[:, cols]))
        plan.append((down_any.at[cols], d.at[cols]))
    copies = [pltpu.make_async_copy(src, dst, sem.at[k]) for k, (src, dst) in enumerate(plan)]
    for copy in copies:
        copy.start()

    pt = p[...].T
    for b in range(16):
        for half in range(2):
            at = (b * 2 + half) * 48
            t[b, half, 96:144] = pt[at : at + 48]
    acc = None
    for k in range(3):
        copies[k].wait()
        part = jnp.dot(
            p[:, k * 512 : k * 512 + 512], w[k * 512 : k * 512 + 512], preferred_element_type=F32
        )
        acc = part if acc is None else acc + part
    embed = acc.astype(BF).astype(F32)
    center = jnp.mean(embed, axis=1, keepdims=True)
    shifted = embed - center
    scale = lax.rsqrt(jnp.mean(shifted * shifted, axis=1, keepdims=True) + 1e-06)
    norm = shifted * scale
    normal[...] = norm
    inverse[...] = scale
    normed = (norm * gain[...]).astype(BF)
    nt = normed.T
    for b in range(16):
        for half in range(2):
            at = b * 2 + half
            t[b, half, 64:96] = nt[at * 32 : at * 32 + 32]
    for j in range(8):
        if j % 4 == 0:
            copies[3 + j // 2].wait()
            copies[4 + j // 2].wait()
        cols = slice(j * 256, j * 256 + 256)
        pre = jnp.dot(normed, u[:, cols], preferred_element_type=F32)
        grad = lax.dot_general(g[...], d[cols], OVER_COLUMNS, preferred_element_type=F32)
        cdf = 0.5 * (1.0 + lax.erf(pre * math.sqrt(0.5)))
        slope = cdf + pre * jnp.exp(-0.5 * pre * pre) * (1.0 / math.sqrt(2.0 * math.pi))
        preact_grad[:, cols] = (grad * slope).astype(BF)
        ht = (pre * cdf).astype(BF).T
        for q in range(4):
            t[j * 2 + q // 2, q % 2, 0:64] = ht[q * 64 : q * 64 + 64]
    c = pos[3]
    mine[...] = t[:, c]
    send[...] = t[:, 1 - c]


def gelu_pass(pos, gain, patches, cotangent, stem_weight, up_weight, down_weight):
    outs = [((256, 2048), BF), ((256, 1024), F32), ((256, 1), F32)]
    return call(
        gelu_pass_body,
        outs + [((16, SHARE, 256), BF)] * 2,
        [
            pltpu.VMEM((1536, 1024), BF),
            pltpu.VMEM((1024, 2048), BF),
            pltpu.VMEM((2048, 1024), BF),
            pltpu.VMEM((16, 2, SHARE, 256), BF),
            pltpu.SemaphoreType.DMA((7,)),
        ],
        "gelu_pass",
        pos,
        gain,
        patches,
        cotangent,
        stem_weight,
        up_weight,
        down_weight,
        limit=48,
        specs=[SMEM] + [VMEM] * 3 + [pl.BlockSpec(memory_space=pl.ANY)] * 3,
        gflop=8,
    )


def norm_back_body(gain, preact_grad, up, cot, normal, inverse, embed_grad):
    grad = lax.dot_general(preact_grad[...], up[...], OVER_COLUMNS, preferred_element_type=F32)
    grad = grad * gain[...]
    norm = normal[...]
    first = jnp.mean(grad, axis=1, keepdims=True)
    second = jnp.mean(grad * norm, axis=1, keepdims=True)
    embed_grad[...] = (
        cot[...].astype(F32) + inverse[...] * (grad - first - norm * second)
    ).astype(BF)


ROWS = 176
SPLIT = 4
CHUNK_X = 512 + SPLIT * 64
CHUNK_Y = (8 - SPLIT) * 64 + 384


def chunk_of(me, pos, rel):
    return lax.rem(me + rel * (1 + 2 * pos[3]), 4)


def dot2(lefts, rights):
    acc = jnp.dot(lefts[0], rights[0], preferred_element_type=F32)
    acc += jnp.dot(lefts[1], rights[1], preferred_element_type=F32)
    return acc.astype(BF)


def columns(ref, starts, width):
    parts = [ref[:, pl.ds(pl.multiple_of(start, LANES), width)] for start in starts]
    return parts[0] if len(parts) == 1 else jnp.concatenate(parts, axis=1)


def terms_x_body(pos, lm, lr, cm, cr, gm, gr, *outs):
    for rel in range(4):
        to = chunk_of(pos[0], pos, rel)
        xh, xl = to // 2, lax.rem(to, 2)
        dst = outs[rel]
        acc = dot2(
            [ref[:, xh, 0:64].reshape(512, 256) for ref in (lm, lr)],
            [columns(ref, [xl * 512], 512) for ref in (cm, cr)],
        )
        for yy in range(4):
            dst[yy, 0:512] = acc[:, yy * 128 : yy * 128 + 128]
        acc = dot2(
            [ref[0:SPLIT, xh, 64:96].reshape(SPLIT * 32, 256) for ref in (lm, lr)],
            [columns(ref, [(yy * 2 + xl) * 256 for yy in range(4)], 256) for ref in (gm, gr)],
        )
        for z in range(SPLIT):
            for yy in range(4):
                for k in range(2):
                    at, col = 512 + z * 64 + k * 32, (yy * 2 + k) * 128
                    dst[yy, at : at + 32] = acc[z * 32 : z * 32 + 32, col : col + 128]


def terms_y_body(pos, lm, lr, gm, gr, em, er, *outs):
    for rel in range(4):
        to = chunk_of(pos[1], pos, rel)
        dst = outs[rel]
        acc = dot2(
            [ref[SPLIT:8, :, 64:96].reshape((8 - SPLIT) * 64, 256) for ref in (lm, lr)],
            [columns(ref, [to * 512], 512) for ref in (gm, gr)],
        )
        for z in range(8 - SPLIT):
            for xx in range(4):
                for k in range(2):
                    row, col = (z * 2 + xx // 2) * 32, (xx % 2 * 2 + k) * 128
                    at = z * 64 + k * 32
                    dst[xx, at : at + 32] = acc[row : row + 32, col : col + 128]
        acc = dot2(
            [ref[:, :, 96:144].reshape(768, 256) for ref in (lm, lr)],
            [columns(ref, [to * 128, 512 + to * 128], 128) for ref in (em, er)],
        )
        for z in range(8):
            for xx in range(4):
                row, col = (z * 2 + xx // 2) * 48, xx % 2 * 128
                at = CHUNK_Y - 384 + z * 48
                dst[xx, at : at + 48] = acc[row : row + 48, col : col + 128]


def pass_on_body(keep, got, out):
    out[...] = (keep[...].astype(F32) + got[...].astype(F32)).astype(BF)


def rings(axes, parts, together):
    result = []
    for p, (axis, (own, keep, ahead, behind)) in enumerate(zip(axes, parts)):
        got = move(ahead, axis, 1)
        near = move(behind, axis, -1)
        if together[p]:
            got, near = lax.optimization_barrier((got, near))
        (total,) = call(
            pass_on_body, [(keep.shape, BF)], [], "pass_on", keep, got, specs=[VMEM, VMEM]
        )
        result += [own, near, move(total, axis, 1)]
    return result


def add3(a, b, c):
    return (a.astype(F32) + b.astype(F32) + c.astype(F32)).astype(BF)


def turn_body(second, pos, own, near, far, *outs):
    for rel in range(4):
        to = chunk_of(pos[second], pos, rel)
        outs[rel][...] = add3(own[to], near[to], far[to])


def reduce_xy(pos, parts):
    sums = rings("xy", parts, (False, True))
    turned = [
        call(
            functools.partial(turn_body, 1 - p),
            [(sums[3 * p].shape[1:], BF)] * 4,
            [],
            "ring_turn_" + "xy"[p],
            pos,
            *sums[3 * p : 3 * p + 3],
        )
        for p in range(2)
    ]
    return rings("yx", turned, (True, True))


def pack_body(*refs):
    out = refs[6]
    x, y = (add3(*(ref[...] for ref in refs[3 * p : 3 * p + 3])) for p in range(2))
    for z in range(8):
        out[z, 0:64] = x[z * 64 : z * 64 + 64]
        up, at = (x, 512 + z * 64) if z < SPLIT else (y, (z - SPLIT) * 64)
        out[z, 64:128] = up[at : at + 64]
        at = CHUNK_Y - 384 + z * 48
        out[z, 128:176] = y[at : at + 48]


def sum_body(got, out):
    total = got[0].astype(F32)
    for k in range(1, 8):
        total += got[k].astype(F32)
    share = total.astype(BF)
    for k in range(8):
        out[k] = share


def unpack_body(got, stem, up, down):
    for y in range(4):
        for xl in range(2):
            piece = got[y * 2 + xl].astype(F32)
            col = (xl * 4 + y) * LANES
            down[:, col : col + LANES] = piece[0:64]
            stem[:, col : col + LANES] = piece[128:176]
            col = (y * 2 + xl) * 256
            up[:, col : col + LANES] = piece[64:96]
            up[:, col + LANES : col + 256] = piece[96:128]


def finish(pieces):
    share = [((8, ROWS, LANES), BF)]
    (packed,) = call(pack_body, share, [], "z_pack", *pieces, specs=[VMEM] * 6)
    got = lax.all_to_all(packed, "z", 0, 0, tiled=True)
    (copies,) = call(sum_body, share, [], "z_sum", got, specs=[VMEM])
    every = lax.all_to_all(copies, ("y", "xl"), 0, 0, tiled=True)
    outs = [((48, 1024), F32), ((32, 2048), F32), ((64, 1024), F32)]
    return call(unpack_body, outs, [], "unpack", every, specs=[VMEM])


def local(patches, stem_weight, ln_gain, up_weight, down_weight, cotangent):
    x = lax.axis_index("xh") * 2 + lax.axis_index("xl")
    pos = jnp.stack([x, lax.axis_index("y"), lax.axis_index("z"), lax.axis_index("c")])
    pos = pos.astype(jnp.int32)

    gain = ln_gain.reshape(1, 1024)
    cot_other = move(cotangent, "c", 0)
    preact_grad, normal, inverse, mine, send = gelu_pass(
        pos, gain, patches, cotangent, stem_weight, up_weight, down_weight
    )
    other = move(send, "c", 0)
    preact_other = move(preact_grad, "c", 0)
    (embed_grad,) = call(
        norm_back_body,
        [((256, 1024), BF)],
        [],
        "norm_back",
        gain,
        preact_grad,
        up_weight,
        cotangent,
        normal,
        inverse,
        specs=[VMEM] * 6,
        limit=16,
        gflop=2,
    )
    embed_other = move(embed_grad, "c", 0)

    left = [v.reshape(8, 2, SHARE, 256) for v in (mine, other)]
    outs_x, outs_y = ([((4, rows, LANES), BF)] * 4 for rows in (CHUNK_X, CHUNK_Y))
    grads = (preact_grad, preact_other)
    part_x = call(
        terms_x_body, outs_x, [], "terms_x", pos, *left, cotangent, cot_other, *grads, limit=16, gflop=2
    )
    embed_other, *part_x = lax.optimization_barrier((embed_other, *part_x))
    part_y = call(
        terms_y_body, outs_y, [], "terms_y", pos, *left, *grads, embed_grad, embed_other, limit=16, gflop=2
    )
    return tuple(finish(reduce_xy(pos, (part_x, part_y))))


def solution(mesh):
    fine = Mesh(mesh.devices.reshape(4, 2, 8, 2, 2), AXES)
    rows = P(("z", "xh", "c"), None)
    in_specs = (P(AXES, None), P(), P(), P(), P(), P(AXES, None))
    return jax.shard_map(
        local, mesh=fine, in_specs=in_specs, out_specs=(rows, rows, rows), check_vma=False
    )
```

```python
import functools
import math

import jax
import jax.numpy as jnp
from jax import lax
from jax.experimental import pallas as pl
from jax.experimental.pallas import tpu as pltpu
from jax.sharding import Mesh, PartitionSpec as P

BF = jnp.bfloat16
F32 = jnp.float32
AXES = ("y", "xl", "z", "xh", "c")
VMEM = pl.BlockSpec(memory_space=pltpu.VMEM)
SMEM = pl.BlockSpec(memory_space=pltpu.SMEM)
LANES = 128
OVER_COLUMNS = (((1,), (1,)), ((), ()))


def move(value, axis, hop):
    pairs = []
    for y in range(4):
        for x in range(4):
            for z in range(8):
                for c in range(2):
                    far = hop * (1 - 2 * c)
                    X = (x + far) % 4 if axis == "x" else x
                    Y = (y + far) % 4 if axis == "y" else y
                    C = 1 - c if axis == "c" else c
                    src = (y * 2 + x % 2) * 32 + z * 4 + (x // 2) * 2 + c
                    dst = (Y * 2 + X % 2) * 32 + z * 4 + (X // 2) * 2 + C
                    pairs.append((src, dst))
    return lax.ppermute(value, AXES, sorted(pairs))


def call(body, outs, scratch, name, *operands, limit=8, specs=None, gflop=0.02):
    return pl.pallas_call(
        body,
        out_shape=[jax.ShapeDtypeStruct(s, d) for s, d in outs],
        in_specs=specs or [SMEM] + [VMEM] * (len(operands) - 1),
        out_specs=[VMEM] * len(outs),
        scratch_shapes=scratch,
        name=name,
        cost_estimate=pl.CostEstimate(
            flops=int(gflop * 1e9), bytes_accessed=1 << 20, transcendentals=0
        ),
        compiler_params=pltpu.CompilerParams(vmem_limit_bytes=limit << 20),
    )(*operands)


SHARE = 144


def gelu_pass_body(
    pos, gain, p, g, stem_any, up_any, down_any,
    preact_grad, normal, inverse, mine, send,
    w, u, d, t, sem,
):
    plan = []
    for k in range(3):
        rows = pl.ds(k * 512, 512)
        plan.append((stem_any.at[rows], w.at[rows]))
    for k in range(2):
        cols = pl.ds(k * 1024, 1024)
        plan.append((up_any.at[:, cols], u.at[:, cols]))
        plan.append((down_any.at[cols], d.at[cols]))
    copies = [pltpu.make_async_copy(src, dst, sem.at[k]) for k, (src, dst) in enumerate(plan)]
    for copy in copies:
        copy.start()

    pt = p[...].T
    for b in range(16):
        for half in range(2):
            at = (b * 2 + half) * 48
            t[b, half, 96:144] = pt[at : at + 48]
    acc = None
    for k in range(3):
        copies[k].wait()
        part = jnp.dot(
            p[:, k * 512 : k * 512 + 512], w[k * 512 : k * 512 + 512], preferred_element_type=F32
        )
        acc = part if acc is None else acc + part
    embed = acc.astype(BF).astype(F32)
    center = jnp.mean(embed, axis=1, keepdims=True)
    shifted = embed - center
    scale = lax.rsqrt(jnp.mean(shifted * shifted, axis=1, keepdims=True) + 1e-06)
    norm = shifted * scale
    normal[...] = norm
    inverse[...] = scale
    normed = (norm * gain[...]).astype(BF)
    nt = normed.T
    for b in range(16):
        for half in range(2):
            at = b * 2 + half
            t[b, half, 64:96] = nt[at * 32 : at * 32 + 32]
    for j in range(8):
        if j % 4 == 0:
            copies[3 + j // 2].wait()
            copies[4 + j // 2].wait()
        cols = slice(j * 256, j * 256 + 256)
        pre = jnp.dot(normed, u[:, cols], preferred_element_type=F32)
        grad = lax.dot_general(g[...], d[cols], OVER_COLUMNS, preferred_element_type=F32)
        cdf = 0.5 * (1.0 + lax.erf(pre * math.sqrt(0.5)))
        slope = cdf + pre * jnp.exp(-0.5 * pre * pre) * (1.0 / math.sqrt(2.0 * math.pi))
        preact_grad[:, cols] = (grad * slope).astype(BF)
        ht = (pre * cdf).astype(BF).T
        for q in range(4):
            t[j * 2 + q // 2, q % 2, 0:64] = ht[q * 64 : q * 64 + 64]
    c = pos[3]
    mine[...] = t[:, c]
    send[...] = t[:, 1 - c]


def gelu_pass(pos, gain, patches, cotangent, stem_weight, up_weight, down_weight):
    outs = [((256, 2048), BF), ((256, 1024), F32), ((256, 1), F32)]
    return call(
        gelu_pass_body,
        outs + [((16, SHARE, 256), BF)] * 2,
        [
            pltpu.VMEM((1536, 1024), BF),
            pltpu.VMEM((1024, 2048), BF),
            pltpu.VMEM((2048, 1024), BF),
            pltpu.VMEM((16, 2, SHARE, 256), BF),
            pltpu.SemaphoreType.DMA((7,)),
        ],
        "gelu_pass",
        pos,
        gain,
        patches,
        cotangent,
        stem_weight,
        up_weight,
        down_weight,
        limit=48,
        specs=[SMEM] + [VMEM] * 3 + [pl.BlockSpec(memory_space=pl.ANY)] * 3,
        gflop=8,
    )


def norm_back_body(gain, preact_grad, up, cot, normal, inverse, embed_grad):
    grad = lax.dot_general(preact_grad[...], up[...], OVER_COLUMNS, preferred_element_type=F32)
    grad = grad * gain[...]
    norm = normal[...]
    first = jnp.mean(grad, axis=1, keepdims=True)
    second = jnp.mean(grad * norm, axis=1, keepdims=True)
    embed_grad[...] = (
        cot[...].astype(F32) + inverse[...] * (grad - first - norm * second)
    ).astype(BF)


ROWS = 176
SPLIT = 5
CHUNK_X = 512 + SPLIT * 64
CHUNK_Y = (8 - SPLIT) * 64 + 384


def chunk_of(me, pos, rel):
    return lax.rem(me + rel * (1 + 2 * pos[3]), 4)


def dot2(lefts, rights):
    left, right = jnp.concatenate(lefts, axis=1), jnp.concatenate(rights, axis=0)
    return jnp.dot(left, right, preferred_element_type=F32).astype(BF)


def columns(ref, starts, width):
    parts = [ref[:, pl.ds(pl.multiple_of(start, LANES), width)] for start in starts]
    return parts[0] if len(parts) == 1 else jnp.concatenate(parts, axis=1)


def terms_x_body(pos, lm, lr, cm, cr, gm, gr, *outs):
    for rel in range(4):
        to = chunk_of(pos[0], pos, rel)
        xh, xl = to // 2, lax.rem(to, 2)
        dst = outs[rel]
        acc = dot2(
            [ref[:, xh, 0:64].reshape(512, 256) for ref in (lm, lr)],
            [columns(ref, [xl * 512], 512) for ref in (cm, cr)],
        )
        for yy in range(4):
            dst[yy, 0:512] = acc[:, yy * 128 : yy * 128 + 128]
        acc = dot2(
            [ref[0:SPLIT, xh, 64:96].reshape(SPLIT * 32, 256) for ref in (lm, lr)],
            [columns(ref, [(yy * 2 + xl) * 256 for yy in range(4)], 256) for ref in (gm, gr)],
        )
        for z in range(SPLIT):
            for yy in range(4):
                for k in range(2):
                    at, col = 512 + z * 64 + k * 32, (yy * 2 + k) * 128
                    dst[yy, at : at + 32] = acc[z * 32 : z * 32 + 32, col : col + 128]


def terms_y_body(pos, lm, lr, gm, gr, em, er, *outs):
    for rel in range(4):
        to = chunk_of(pos[1], pos, rel)
        dst = outs[rel]
        acc = dot2(
            [ref[SPLIT:8, :, 64:96].reshape((8 - SPLIT) * 64, 256) for ref in (lm, lr)],
            [columns(ref, [to * 512], 512) for ref in (gm, gr)],
        )
        for z in range(8 - SPLIT):
            for xx in range(4):
                for k in range(2):
                    row, col = (z * 2 + xx // 2) * 32, (xx % 2 * 2 + k) * 128
                    at = z * 64 + k * 32
                    dst[xx, at : at + 32] = acc[row : row + 32, col : col + 128]
        acc = dot2(
            [ref[:, :, 96:144].reshape(768, 256) for ref in (lm, lr)],
            [columns(ref, [to * 128, 512 + to * 128], 128) for ref in (em, er)],
        )
        for z in range(8):
            for xx in range(4):
                row, col = (z * 2 + xx // 2) * 48, xx % 2 * 128
                at = CHUNK_Y - 384 + z * 48
                dst[xx, at : at + 48] = acc[row : row + 48, col : col + 128]


def pass_on_body(keep, got, out):
    out[...] = (keep[...].astype(F32) + got[...].astype(F32)).astype(BF)


def rings(axes, parts):
    result = []
    for p, (axis, (own, keep, ahead, behind)) in enumerate(zip(axes, parts)):
        got = move(ahead, axis, 1)
        near = move(behind, axis, -1)
        if p == 1:
            got, near = lax.optimization_barrier((got, near))
        (total,) = call(
            pass_on_body, [(keep.shape, BF)], [], "pass_on", keep, got, specs=[VMEM, VMEM]
        )
        result += [own, near, move(total, axis, 1)]
    return result


def add3(a, b, c):
    return (a.astype(F32) + b.astype(F32) + c.astype(F32)).astype(BF)


def turn_body(second, pos, own, near, far, *outs):
    for rel in range(4):
        to = chunk_of(pos[second], pos, rel)
        outs[rel][...] = add3(own[to], near[to], far[to])


def reduce_xy(pos, parts):
    sums = rings("xy", parts)
    turned = [
        call(
            functools.partial(turn_body, 1 - p),
            [(sums[3 * p].shape[1:], BF)] * 4,
            [],
            "ring_turn_" + "xy"[p],
            pos,
            *sums[3 * p : 3 * p + 3],
        )
        for p in range(2)
    ]
    return rings("yx", turned)


def pack_body(*refs):
    out = refs[6]
    x, y = (add3(*(ref[...] for ref in refs[3 * p : 3 * p + 3])) for p in range(2))
    for z in range(8):
        out[z, 0:64] = x[z * 64 : z * 64 + 64]
        up, at = (x, 512 + z * 64) if z < SPLIT else (y, (z - SPLIT) * 64)
        out[z, 64:128] = up[at : at + 64]
        at = CHUNK_Y - 384 + z * 48
        out[z, 128:176] = y[at : at + 48]


def sum_body(got, out):
    total = got[0].astype(F32)
    for k in range(1, 8):
        total += got[k].astype(F32)
    share = total.astype(BF)
    for k in range(8):
        out[k] = share


def unpack_body(got, stem, up, down):
    for y in range(4):
        for xl in range(2):
            piece = got[y * 2 + xl].astype(F32)
            col = (xl * 4 + y) * LANES
            down[:, col : col + LANES] = piece[0:64]
            stem[:, col : col + LANES] = piece[128:176]
            col = (y * 2 + xl) * 256
            up[:, col : col + LANES] = piece[64:96]
            up[:, col + LANES : col + 256] = piece[96:128]


def finish(pieces):
    share = [((8, ROWS, LANES), BF)]
    (packed,) = call(pack_body, share, [], "z_pack", *pieces, specs=[VMEM] * 6)
    got = lax.all_to_all(packed, "z", 0, 0, tiled=True)
    (copies,) = call(sum_body, share, [], "z_sum", got, specs=[VMEM])
    every = lax.all_to_all(copies, ("y", "xl"), 0, 0, tiled=True)
    outs = [((48, 1024), F32), ((32, 2048), F32), ((64, 1024), F32)]
    return call(unpack_body, outs, [], "unpack", every, specs=[VMEM])


def local(patches, stem_weight, ln_gain, up_weight, down_weight, cotangent):
    x = lax.axis_index("xh") * 2 + lax.axis_index("xl")
    pos = jnp.stack([x, lax.axis_index("y"), lax.axis_index("z"), lax.axis_index("c")])
    pos = pos.astype(jnp.int32)

    gain = ln_gain.reshape(1, 1024)
    cot_other = move(cotangent, "c", 0)
    preact_grad, normal, inverse, mine, send = gelu_pass(
        pos, gain, patches, cotangent, stem_weight, up_weight, down_weight
    )
    send, cot_other = lax.optimization_barrier((send, cot_other))
    other = move(send, "c", 0)
    preact_other = move(preact_grad, "c", 0)
    (embed_grad,) = call(
        norm_back_body,
        [((256, 1024), BF)],
        [],
        "norm_back",
        gain,
        preact_grad,
        up_weight,
        cotangent,
        normal,
        inverse,
        specs=[VMEM] * 6,
        limit=16,
        gflop=2,
    )
    embed_other = move(embed_grad, "c", 0)

    left = [v.reshape(8, 2, SHARE, 256) for v in (mine, other)]
    outs_x, outs_y = ([((4, rows, LANES), BF)] * 4 for rows in (CHUNK_X, CHUNK_Y))
    grads = (preact_grad, preact_other)
    part_x = call(
        terms_x_body, outs_x, [], "terms_x", pos, *left, cotangent, cot_other, *grads, limit=16, gflop=2
    )
    embed_other, *part_x = lax.optimization_barrier((embed_other, *part_x))
    part_y = call(
        terms_y_body, outs_y, [], "terms_y", pos, *left, *grads, embed_grad, embed_other, limit=16, gflop=2
    )
    return tuple(finish(reduce_xy(pos, (part_x, part_y))))


def solution(mesh):
    fine = Mesh(mesh.devices.reshape(4, 2, 8, 2, 2), AXES)
    rows = P(("z", "xh", "c"), None)
    in_specs = (P(AXES, None), P(), P(), P(), P(), P(AXES, None))
    return jax.shard_map(
        local, mesh=fine, in_specs=in_specs, out_specs=(rows, rows, rows), check_vma=False
    )
```

```python
import functools
import math

import jax
import jax.numpy as jnp
from jax import lax
from jax.experimental import pallas as pl
from jax.experimental.pallas import tpu as pltpu
from jax.sharding import Mesh, PartitionSpec as P

BF = jnp.bfloat16
F32 = jnp.float32
AXES = ("y", "xl", "z", "xh", "c")
VMEM = pl.BlockSpec(memory_space=pltpu.VMEM)
SMEM = pl.BlockSpec(memory_space=pltpu.SMEM)
LANES = 128
OVER_COLUMNS = (((1,), (1,)), ((), ()))


def move(value, axis, hop):
    pairs = []
    for y in range(4):
        for x in range(4):
            for z in range(8):
                for c in range(2):
                    far = hop * (1 - 2 * c)
                    X = (x + far) % 4 if axis == "x" else x
                    Y = (y + far) % 4 if axis == "y" else y
                    C = 1 - c if axis == "c" else c
                    src = (y * 2 + x % 2) * 32 + z * 4 + (x // 2) * 2 + c
                    dst = (Y * 2 + X % 2) * 32 + z * 4 + (X // 2) * 2 + C
                    pairs.append((src, dst))
    return lax.ppermute(value, AXES, sorted(pairs))


def call(body, outs, scratch, name, *operands, limit=8, specs=None, gflop=0.02):
    return pl.pallas_call(
        body,
        out_shape=[jax.ShapeDtypeStruct(s, d) for s, d in outs],
        in_specs=specs or [SMEM] + [VMEM] * (len(operands) - 1),
        out_specs=[VMEM] * len(outs),
        scratch_shapes=scratch,
        name=name,
        cost_estimate=pl.CostEstimate(
            flops=int(gflop * 1e9), bytes_accessed=1 << 20, transcendentals=0
        ),
        compiler_params=pltpu.CompilerParams(vmem_limit_bytes=limit << 20),
    )(*operands)


SHARE = 96


def turn_patches_body(pos, p, mine, send, t):
    pt = p[...].T
    for b in range(16):
        for half in range(2):
            at = (b * 2 + half) * 48
            t[b, half] = pt[at : at + 48]
    c = pos[3]
    mine[...] = t[:, c]
    send[...] = t[:, 1 - c]


def gelu_pass_body(
    pos, gain, p, g, stem_any, up_any, down_any,
    preact_grad, normal, inverse, mine, send,
    w, u, d, t, sem,
):
    plan = []
    for k in range(3):
        rows = pl.ds(k * 512, 512)
        plan.append((stem_any.at[rows], w.at[rows]))
    for k in range(2):
        cols = pl.ds(k * 1024, 1024)
        plan.append((up_any.at[:, cols], u.at[:, cols]))
        plan.append((down_any.at[cols], d.at[cols]))
    copies = [pltpu.make_async_copy(src, dst, sem.at[k]) for k, (src, dst) in enumerate(plan)]
    for copy in copies:
        copy.start()

    acc = None
    for k in range(3):
        copies[k].wait()
        part = jnp.dot(
            p[:, k * 512 : k * 512 + 512], w[k * 512 : k * 512 + 512], preferred_element_type=F32
        )
        acc = part if acc is None else acc + part
    embed = acc.astype(BF).astype(F32)
    center = jnp.mean(embed, axis=1, keepdims=True)
    shifted = embed - center
    scale = lax.rsqrt(jnp.mean(shifted * shifted, axis=1, keepdims=True) + 1e-06)
    norm = shifted * scale
    normal[...] = norm
    inverse[...] = scale
    normed = (norm * gain[...]).astype(BF)
    nt = normed.T
    for b in range(16):
        for half in range(2):
            at = b * 2 + half
            t[b, half, 64:96] = nt[at * 32 : at * 32 + 32]
    for j in range(8):
        if j % 4 == 0:
            copies[3 + j // 2].wait()
            copies[4 + j // 2].wait()
        cols = slice(j * 256, j * 256 + 256)
        pre = jnp.dot(normed, u[:, cols], preferred_element_type=F32)
        grad = lax.dot_general(g[...], d[cols], OVER_COLUMNS, preferred_element_type=F32)
        cdf = 0.5 * (1.0 + lax.erf(pre * math.sqrt(0.5)))
        slope = cdf + pre * jnp.exp(-0.5 * pre * pre) * (1.0 / math.sqrt(2.0 * math.pi))
        preact_grad[:, cols] = (grad * slope).astype(BF)
        ht = (pre * cdf).astype(BF).T
        for q in range(4):
            t[j * 2 + q // 2, q % 2, 0:64] = ht[q * 64 : q * 64 + 64]
    c = pos[3]
    mine[...] = t[:, c]
    send[...] = t[:, 1 - c]


def gelu_pass(pos, gain, patches, cotangent, stem_weight, up_weight, down_weight):
    outs = [((256, 2048), BF), ((256, 1024), F32), ((256, 1), F32)]
    return call(
        gelu_pass_body,
        outs + [((16, SHARE, 256), BF)] * 2,
        [
            pltpu.VMEM((1536, 1024), BF),
            pltpu.VMEM((1024, 2048), BF),
            pltpu.VMEM((2048, 1024), BF),
            pltpu.VMEM((16, 2, SHARE, 256), BF),
            pltpu.SemaphoreType.DMA((7,)),
        ],
        "gelu_pass",
        pos,
        gain,
        patches,
        cotangent,
        stem_weight,
        up_weight,
        down_weight,
        limit=48,
        specs=[SMEM] + [VMEM] * 3 + [pl.BlockSpec(memory_space=pl.ANY)] * 3,
        gflop=8,
    )


def norm_back_body(gain, preact_grad, up, cot, normal, inverse, embed_grad):
    grad = lax.dot_general(preact_grad[...], up[...], OVER_COLUMNS, preferred_element_type=F32)
    grad = grad * gain[...]
    norm = normal[...]
    first = jnp.mean(grad, axis=1, keepdims=True)
    second = jnp.mean(grad * norm, axis=1, keepdims=True)
    embed_grad[...] = (
        cot[...].astype(F32) + inverse[...] * (grad - first - norm * second)
    ).astype(BF)


ROWS = 176
SPLIT = 4
CHUNK_X = 512 + SPLIT * 64
CHUNK_Y = (8 - SPLIT) * 64 + 384


def chunk_of(me, pos, rel):
    return lax.rem(me + rel * (1 + 2 * pos[3]), 4)


def dot2(lefts, rights):
    left, right = jnp.concatenate(lefts, axis=1), jnp.concatenate(rights, axis=0)
    return jnp.dot(left, right, preferred_element_type=F32).astype(BF)


def columns(ref, starts, width):
    parts = [ref[:, pl.ds(pl.multiple_of(start, LANES), width)] for start in starts]
    return parts[0] if len(parts) == 1 else jnp.concatenate(parts, axis=1)


def terms_x_body(pos, lm, lr, cm, cr, gm, gr, *outs):
    for rel in range(4):
        to = chunk_of(pos[0], pos, rel)
        xh, xl = to // 2, lax.rem(to, 2)
        dst = outs[rel]
        acc = dot2(
            [ref[:, xh, 0:64].reshape(512, 256) for ref in (lm, lr)],
            [columns(ref, [xl * 512], 512) for ref in (cm, cr)],
        )
        for yy in range(4):
            dst[yy, 0:512] = acc[:, yy * 128 : yy * 128 + 128]
        acc = dot2(
            [ref[0:SPLIT, xh, 64:96].reshape(SPLIT * 32, 256) for ref in (lm, lr)],
            [columns(ref, [(yy * 2 + xl) * 256 for yy in range(4)], 256) for ref in (gm, gr)],
        )
        for z in range(SPLIT):
            for yy in range(4):
                for k in range(2):
                    at, col = 512 + z * 64 + k * 32, (yy * 2 + k) * 128
                    dst[yy, at : at + 32] = acc[z * 32 : z * 32 + 32, col : col + 128]


def terms_y_body(pos, lm, lr, pm, pr, gm, gr, em, er, *outs):
    for rel in range(4):
        to = chunk_of(pos[1], pos, rel)
        dst = outs[rel]
        acc = dot2(
            [ref[SPLIT:8, :, 64:96].reshape((8 - SPLIT) * 64, 256) for ref in (lm, lr)],
            [columns(ref, [to * 512], 512) for ref in (gm, gr)],
        )
        for z in range(8 - SPLIT):
            for xx in range(4):
                for k in range(2):
                    row, col = (z * 2 + xx // 2) * 32, (xx % 2 * 2 + k) * 128
                    at = z * 64 + k * 32
                    dst[xx, at : at + 32] = acc[row : row + 32, col : col + 128]
        acc = dot2(
            [ref[...].reshape(768, 256) for ref in (pm, pr)],
            [columns(ref, [to * 128, 512 + to * 128], 128) for ref in (em, er)],
        )
        for z in range(8):
            for xx in range(4):
                row, col = (z * 2 + xx // 2) * 48, xx % 2 * 128
                at = CHUNK_Y - 384 + z * 48
                dst[xx, at : at + 48] = acc[row : row + 48, col : col + 128]


def pass_on_body(keep, got, out):
    out[...] = (keep[...].astype(F32) + got[...].astype(F32)).astype(BF)


def rings(axes, parts):
    result = []
    for p, (axis, (own, keep, ahead, behind)) in enumerate(zip(axes, parts)):
        got = move(ahead, axis, 1)
        near = move(behind, axis, -1)
        if p == 1:
            got, near = lax.optimization_barrier((got, near))
        (total,) = call(
            pass_on_body, [(keep.shape, BF)], [], "pass_on", keep, got, specs=[VMEM, VMEM]
        )
        result += [own, near, move(total, axis, 1)]
    return result


def add3(a, b, c):
    return (a.astype(F32) + b.astype(F32) + c.astype(F32)).astype(BF)


def turn_body(second, pos, own, near, far, *outs):
    for rel in range(4):
        to = chunk_of(pos[second], pos, rel)
        outs[rel][...] = add3(own[to], near[to], far[to])


def reduce_xy(pos, parts):
    sums = rings("xy", parts)
    turned = [
        call(
            functools.partial(turn_body, 1 - p),
            [(sums[3 * p].shape[1:], BF)] * 4,
            [],
            "ring_turn_" + "xy"[p],
            pos,
            *sums[3 * p : 3 * p + 3],
        )
        for p in range(2)
    ]
    return rings("yx", turned)


def pack_body(*refs):
    out = refs[6]
    x, y = (add3(*(ref[...] for ref in refs[3 * p : 3 * p + 3])) for p in range(2))
    for z in range(8):
        out[z, 0:64] = x[z * 64 : z * 64 + 64]
        up, at = (x, 512 + z * 64) if z < SPLIT else (y, (z - SPLIT) * 64)
        out[z, 64:128] = up[at : at + 64]
        at = CHUNK_Y - 384 + z * 48
        out[z, 128:176] = y[at : at + 48]


def sum_body(got, out):
    total = got[0].astype(F32)
    for k in range(1, 8):
        total += got[k].astype(F32)
    share = total.astype(BF)
    for k in range(8):
        out[k] = share


def unpack_body(got, stem, up, down):
    for y in range(4):
        for xl in range(2):
            piece = got[y * 2 + xl].astype(F32)
            col = (xl * 4 + y) * LANES
            down[:, col : col + LANES] = piece[0:64]
            stem[:, col : col + LANES] = piece[128:176]
            col = (y * 2 + xl) * 256
            up[:, col : col + LANES] = piece[64:96]
            up[:, col + LANES : col + 256] = piece[96:128]


def finish(pieces):
    share = [((8, ROWS, LANES), BF)]
    (packed,) = call(pack_body, share, [], "z_pack", *pieces, specs=[VMEM] * 6)
    got = lax.all_to_all(packed, "z", 0, 0, tiled=True)
    (copies,) = call(sum_body, share, [], "z_sum", got, specs=[VMEM])
    every = lax.all_to_all(copies, ("y", "xl"), 0, 0, tiled=True)
    outs = [((48, 1024), F32), ((32, 2048), F32), ((64, 1024), F32)]
    return call(unpack_body, outs, [], "unpack", every, specs=[VMEM])


def local(patches, stem_weight, ln_gain, up_weight, down_weight, cotangent):
    x = lax.axis_index("xh") * 2 + lax.axis_index("xl")
    pos = jnp.stack([x, lax.axis_index("y"), lax.axis_index("z"), lax.axis_index("c")])
    pos = pos.astype(jnp.int32)

    gain = ln_gain.reshape(1, 1024)
    patches_mine, patches_send = call(
        turn_patches_body,
        [((16, 48, 256), BF)] * 2,
        [pltpu.VMEM((16, 2, 48, 256), BF)],
        "turn_patches",
        pos,
        patches,
        limit=12,
        gflop=2,
    )
    patches_other = move(patches_send, "c", 0)
    cot_other = move(cotangent, "c", 0)
    preact_grad, normal, inverse, mine, send = gelu_pass(
        pos, gain, patches, cotangent, stem_weight, up_weight, down_weight
    )
    send, cot_other, patches_other = lax.optimization_barrier((send, cot_other, patches_other))
    other = move(send, "c", 0)
    preact_other = move(preact_grad, "c", 0)
    (embed_grad,) = call(
        norm_back_body,
        [((256, 1024), BF)],
        [],
        "norm_back",
        gain,
        preact_grad,
        up_weight,
        cotangent,
        normal,
        inverse,
        specs=[VMEM] * 6,
        limit=16,
        gflop=2,
    )
    embed_other = move(embed_grad, "c", 0)

    left = [v.reshape(8, 2, SHARE, 256) for v in (mine, other)]
    outs_x, outs_y = ([((4, rows, LANES), BF)] * 4 for rows in (CHUNK_X, CHUNK_Y))
    grads = (preact_grad, preact_other)
    part_x = call(
        terms_x_body, outs_x, [], "terms_x", pos, *left, cotangent, cot_other, *grads, limit=16, gflop=2
    )
    embed_other, *part_x = lax.optimization_barrier((embed_other, *part_x))
    part_y = call(
        terms_y_body, outs_y, [], "terms_y", pos, *left, patches_mine, patches_other, *grads, embed_grad, embed_other, limit=16, gflop=2
    )
    return tuple(finish(reduce_xy(pos, (part_x, part_y))))


def solution(mesh):
    fine = Mesh(mesh.devices.reshape(4, 2, 8, 2, 2), AXES)
    rows = P(("z", "xh", "c"), None)
    in_specs = (P(AXES, None), P(), P(), P(), P(), P(AXES, None))
    return jax.shard_map(
        local, mesh=fine, in_specs=in_specs, out_specs=(rows, rows, rows), check_vma=False
    )
```

```python
import functools
import math

import jax
import jax.numpy as jnp
from jax import lax
from jax.experimental import pallas as pl
from jax.experimental.pallas import tpu as pltpu
from jax.sharding import Mesh, PartitionSpec as P

BF = jnp.bfloat16
F32 = jnp.float32
AXES = ("y", "xl", "z", "xh", "c")
VMEM = pl.BlockSpec(memory_space=pltpu.VMEM)
SMEM = pl.BlockSpec(memory_space=pltpu.SMEM)
LANES = 128
OVER_COLUMNS = (((1,), (1,)), ((), ()))


def move(value, axis, hop):
    pairs = []
    for y in range(4):
        for x in range(4):
            for z in range(8):
                for c in range(2):
                    far = hop * (1 - 2 * c)
                    X = (x + far) % 4 if axis == "x" else x
                    Y = (y + far) % 4 if axis == "y" else y
                    C = 1 - c if axis == "c" else c
                    src = (y * 2 + x % 2) * 32 + z * 4 + (x // 2) * 2 + c
                    dst = (Y * 2 + X % 2) * 32 + z * 4 + (X // 2) * 2 + C
                    pairs.append((src, dst))
    return lax.ppermute(value, AXES, sorted(pairs))


def call(body, outs, scratch, name, *operands, limit=8, specs=None, gflop=0.02):
    return pl.pallas_call(
        body,
        out_shape=[jax.ShapeDtypeStruct(s, d) for s, d in outs],
        in_specs=specs or [SMEM] + [VMEM] * (len(operands) - 1),
        out_specs=[VMEM] * len(outs),
        scratch_shapes=scratch,
        name=name,
        cost_estimate=pl.CostEstimate(
            flops=int(gflop * 1e9), bytes_accessed=1 << 20, transcendentals=0
        ),
        compiler_params=pltpu.CompilerParams(vmem_limit_bytes=limit << 20),
    )(*operands)


SHARE = 96


def turn_patches_body(pos, p, mine, send, t):
    pt = p[...].T
    for b in range(16):
        for half in range(2):
            at = (b * 2 + half) * 48
            t[b, half] = pt[at : at + 48]
    c = pos[3]
    mine[...] = t[:, c]
    send[...] = t[:, 1 - c]


def gelu_pass_body(
    pos, gain, p, g, w, up_any, down_any,
    preact_grad, normal, inverse, mine, send,
    u, d, t, sem,
):
    plan = []
    for k in range(2):
        cols = pl.ds(k * 1024, 1024)
        plan.append((up_any.at[:, cols], u.at[:, cols]))
        plan.append((down_any.at[cols], d.at[cols]))
    copies = [pltpu.make_async_copy(src, dst, sem.at[k]) for k, (src, dst) in enumerate(plan)]
    for copy in copies:
        copy.start()

    acc = jnp.dot(p[...], w[...], preferred_element_type=F32)
    embed = acc.astype(BF).astype(F32)
    center = jnp.mean(embed, axis=1, keepdims=True)
    shifted = embed - center
    scale = lax.rsqrt(jnp.mean(shifted * shifted, axis=1, keepdims=True) + 1e-06)
    norm = shifted * scale
    normal[...] = norm
    inverse[...] = scale
    normed = (norm * gain[...]).astype(BF)
    nt = normed.T
    for b in range(16):
        for half in range(2):
            at = b * 2 + half
            t[b, half, 64:96] = nt[at * 32 : at * 32 + 32]
    for j in range(8):
        if j % 4 == 0:
            copies[j // 2].wait()
            copies[j // 2 + 1].wait()
        cols = slice(j * 256, j * 256 + 256)
        pre = jnp.dot(normed, u[:, cols], preferred_element_type=F32)
        grad = lax.dot_general(g[...], d[cols], OVER_COLUMNS, preferred_element_type=F32)
        cdf = 0.5 * (1.0 + lax.erf(pre * math.sqrt(0.5)))
        slope = cdf + pre * jnp.exp(-0.5 * pre * pre) * (1.0 / math.sqrt(2.0 * math.pi))
        preact_grad[:, cols] = (grad * slope).astype(BF)
        ht = (pre * cdf).astype(BF).T
        for q in range(4):
            t[j * 2 + q // 2, q % 2, 0:64] = ht[q * 64 : q * 64 + 64]
    c = pos[3]
    mine[...] = t[:, c]
    send[...] = t[:, 1 - c]


def gelu_pass(pos, gain, patches, cotangent, stem_weight, up_weight, down_weight):
    outs = [((256, 2048), BF), ((256, 1024), F32), ((256, 1), F32)]
    return call(
        gelu_pass_body,
        outs + [((16, SHARE, 256), BF)] * 2,
        [
            pltpu.VMEM((1024, 2048), BF),
            pltpu.VMEM((2048, 1024), BF),
            pltpu.VMEM((16, 2, SHARE, 256), BF),
            pltpu.SemaphoreType.DMA((4,)),
        ],
        "gelu_pass",
        pos,
        gain,
        patches,
        cotangent,
        stem_weight,
        up_weight,
        down_weight,
        limit=46,
        specs=[SMEM] + [VMEM] * 4 + [pl.BlockSpec(memory_space=pl.ANY)] * 2,
        gflop=8,
    )


def norm_back_body(gain, preact_grad, up, cot, normal, inverse, embed_grad):
    grad = lax.dot_general(preact_grad[...], up[...], OVER_COLUMNS, preferred_element_type=F32)
    grad = grad * gain[...]
    norm = normal[...]
    first = jnp.mean(grad, axis=1, keepdims=True)
    second = jnp.mean(grad * norm, axis=1, keepdims=True)
    embed_grad[...] = (
        cot[...].astype(F32) + inverse[...] * (grad - first - norm * second)
    ).astype(BF)


ROWS = 176
SPLIT = 4
CHUNK_X = 512 + SPLIT * 64
CHUNK_Y = (8 - SPLIT) * 64 + 384


def chunk_of(me, pos, rel):
    return lax.rem(me + rel * (1 + 2 * pos[3]), 4)


def dot2(lefts, rights):
    left, right = jnp.concatenate(lefts, axis=1), jnp.concatenate(rights, axis=0)
    return jnp.dot(left, right, preferred_element_type=F32).astype(BF)


def columns(ref, starts, width):
    parts = [ref[:, pl.ds(pl.multiple_of(start, LANES), width)] for start in starts]
    return parts[0] if len(parts) == 1 else jnp.concatenate(parts, axis=1)


def terms_x_body(pos, lm, lr, cm, cr, gm, gr, *outs):
    for rel in range(4):
        to = chunk_of(pos[0], pos, rel)
        xh, xl = to // 2, lax.rem(to, 2)
        dst = outs[rel]
        acc = dot2(
            [ref[:, xh, 0:64].reshape(512, 256) for ref in (lm, lr)],
            [columns(ref, [xl * 512], 512) for ref in (cm, cr)],
        )
        for yy in range(4):
            dst[yy, 0:512] = acc[:, yy * 128 : yy * 128 + 128]
        acc = dot2(
            [ref[0:SPLIT, xh, 64:96].reshape(SPLIT * 32, 256) for ref in (lm, lr)],
            [columns(ref, [(yy * 2 + xl) * 256 for yy in range(4)], 256) for ref in (gm, gr)],
        )
        for z in range(SPLIT):
            for yy in range(4):
                for k in range(2):
                    at, col = 512 + z * 64 + k * 32, (yy * 2 + k) * 128
                    dst[yy, at : at + 32] = acc[z * 32 : z * 32 + 32, col : col + 128]


def terms_y_body(pos, lm, lr, pm, pr, gm, gr, em, er, *outs):
    for rel in range(4):
        to = chunk_of(pos[1], pos, rel)
        dst = outs[rel]
        acc = dot2(
            [ref[SPLIT:8, :, 64:96].reshape((8 - SPLIT) * 64, 256) for ref in (lm, lr)],
            [columns(ref, [to * 512], 512) for ref in (gm, gr)],
        )
        for z in range(8 - SPLIT):
            for xx in range(4):
                for k in range(2):
                    row, col = (z * 2 + xx // 2) * 32, (xx % 2 * 2 + k) * 128
                    at = z * 64 + k * 32
                    dst[xx, at : at + 32] = acc[row : row + 32, col : col + 128]
        acc = dot2(
            [ref[...].reshape(768, 256) for ref in (pm, pr)],
            [columns(ref, [to * 128, 512 + to * 128], 128) for ref in (em, er)],
        )
        for z in range(8):
            for xx in range(4):
                row, col = (z * 2 + xx // 2) * 48, xx % 2 * 128
                at = CHUNK_Y - 384 + z * 48
                dst[xx, at : at + 48] = acc[row : row + 48, col : col + 128]


def pass_on_body(keep, got, out):
    out[...] = (keep[...].astype(F32) + got[...].astype(F32)).astype(BF)


def rings(axes, parts):
    result = []
    for p, (axis, (own, keep, ahead, behind)) in enumerate(zip(axes, parts)):
        got = move(ahead, axis, 1)
        near = move(behind, axis, -1)
        if p == 1:
            got, near = lax.optimization_barrier((got, near))
        (total,) = call(
            pass_on_body, [(keep.shape, BF)], [], "pass_on", keep, got, specs=[VMEM, VMEM]
        )
        result += [own, near, move(total, axis, 1)]
    return result


def add3(a, b, c):
    return (a.astype(F32) + b.astype(F32) + c.astype(F32)).astype(BF)


def turn_body(second, pos, own, near, far, *outs):
    for rel in range(4):
        to = chunk_of(pos[second], pos, rel)
        outs[rel][...] = add3(own[to], near[to], far[to])


def reduce_xy(pos, parts):
    sums = rings("xy", parts)
    turned = [
        call(
            functools.partial(turn_body, 1 - p),
            [(sums[3 * p].shape[1:], BF)] * 4,
            [],
            "ring_turn_" + "xy"[p],
            pos,
            *sums[3 * p : 3 * p + 3],
        )
        for p in range(2)
    ]
    return rings("yx", turned)


def pack_body(*refs):
    out = refs[6]
    x, y = (add3(*(ref[...] for ref in refs[3 * p : 3 * p + 3])) for p in range(2))
    for z in range(8):
        out[z, 0:64] = x[z * 64 : z * 64 + 64]
        up, at = (x, 512 + z * 64) if z < SPLIT else (y, (z - SPLIT) * 64)
        out[z, 64:128] = up[at : at + 64]
        at = CHUNK_Y - 384 + z * 48
        out[z, 128:176] = y[at : at + 48]


def sum_body(got, out):
    total = got[0].astype(F32)
    for k in range(1, 8):
        total += got[k].astype(F32)
    share = total.astype(BF)
    for k in range(8):
        out[k] = share


def unpack_body(got, stem, up, down):
    for y in range(4):
        for xl in range(2):
            piece = got[y * 2 + xl].astype(F32)
            col = (xl * 4 + y) * LANES
            down[:, col : col + LANES] = piece[0:64]
            stem[:, col : col + LANES] = piece[128:176]
            col = (y * 2 + xl) * 256
            up[:, col : col + LANES] = piece[64:96]
            up[:, col + LANES : col + 256] = piece[96:128]


def finish(pieces):
    share = [((8, ROWS, LANES), BF)]
    (packed,) = call(pack_body, share, [], "z_pack", *pieces, specs=[VMEM] * 6)
    got = lax.all_to_all(packed, "z", 0, 0, tiled=True)
    (copies,) = call(sum_body, share, [], "z_sum", got, specs=[VMEM])
    every = lax.all_to_all(copies, ("y", "xl"), 0, 0, tiled=True)
    outs = [((48, 1024), F32), ((32, 2048), F32), ((64, 1024), F32)]
    return call(unpack_body, outs, [], "unpack", every, specs=[VMEM])


def local(patches, stem_weight, ln_gain, up_weight, down_weight, cotangent):
    x = lax.axis_index("xh") * 2 + lax.axis_index("xl")
    pos = jnp.stack([x, lax.axis_index("y"), lax.axis_index("z"), lax.axis_index("c")])
    pos = pos.astype(jnp.int32)

    gain = ln_gain.reshape(1, 1024)
    patches_mine, patches_send = call(
        turn_patches_body,
        [((16, 48, 256), BF)] * 2,
        [pltpu.VMEM((16, 2, 48, 256), BF)],
        "turn_patches",
        pos,
        patches,
        limit=12,
        gflop=2,
    )
    patches_other = move(patches_send, "c", 0)
    cot_other = move(cotangent, "c", 0)
    preact_grad, normal, inverse, mine, send = gelu_pass(
        pos, gain, patches, cotangent, stem_weight, up_weight, down_weight
    )
    send, cot_other, patches_other = lax.optimization_barrier((send, cot_other, patches_other))
    other = move(send, "c", 0)
    preact_other = move(preact_grad, "c", 0)
    (embed_grad,) = call(
        norm_back_body,
        [((256, 1024), BF)],
        [],
        "norm_back",
        gain,
        preact_grad,
        up_weight,
        cotangent,
        normal,
        inverse,
        specs=[VMEM] * 6,
        limit=16,
        gflop=2,
    )
    embed_other = move(embed_grad, "c", 0)

    left = [v.reshape(8, 2, SHARE, 256) for v in (mine, other)]
    outs_x, outs_y = ([((4, rows, LANES), BF)] * 4 for rows in (CHUNK_X, CHUNK_Y))
    grads = (preact_grad, preact_other)
    part_x = call(
        terms_x_body, outs_x, [], "terms_x", pos, *left, cotangent, cot_other, *grads, limit=16, gflop=2
    )
    embed_other, *part_x = lax.optimization_barrier((embed_other, *part_x))
    part_y = call(
        terms_y_body, outs_y, [], "terms_y", pos, *left, patches_mine, patches_other, *grads, embed_grad, embed_other, limit=16, gflop=2
    )
    return tuple(finish(reduce_xy(pos, (part_x, part_y))))


def solution(mesh):
    fine = Mesh(mesh.devices.reshape(4, 2, 8, 2, 2), AXES)
    rows = P(("z", "xh", "c"), None)
    in_specs = (P(AXES, None), P(), P(), P(), P(), P(AXES, None))
    return jax.shard_map(
        local, mesh=fine, in_specs=in_specs, out_specs=(rows, rows, rows), check_vma=False
    )
```

```python
import functools
import math

import jax
import jax.numpy as jnp
from jax import lax
from jax.experimental import pallas as pl
from jax.experimental.pallas import tpu as pltpu
from jax.sharding import Mesh, PartitionSpec as P

BF = jnp.bfloat16
F32 = jnp.float32
AXES = ("y", "xl", "z", "xh", "c")
VMEM = pl.BlockSpec(memory_space=pltpu.VMEM)
SMEM = pl.BlockSpec(memory_space=pltpu.SMEM)
LANES = 128
OVER_COLUMNS = (((1,), (1,)), ((), ()))


def move(value, axis, hop):
    pairs = []
    for y in range(4):
        for x in range(4):
            for z in range(8):
                for c in range(2):
                    far = hop * (1 - 2 * c)
                    X = (x + far) % 4 if axis == "x" else x
                    Y = (y + far) % 4 if axis == "y" else y
                    C = 1 - c if axis == "c" else c
                    src = (y * 2 + x % 2) * 32 + z * 4 + (x // 2) * 2 + c
                    dst = (Y * 2 + X % 2) * 32 + z * 4 + (X // 2) * 2 + C
                    pairs.append((src, dst))
    return lax.ppermute(value, AXES, sorted(pairs))


def call(body, outs, scratch, name, *operands, limit=8, specs=None, gflop=0.02):
    return pl.pallas_call(
        body,
        out_shape=[jax.ShapeDtypeStruct(s, d) for s, d in outs],
        in_specs=specs or [SMEM] + [VMEM] * (len(operands) - 1),
        out_specs=[VMEM] * len(outs),
        scratch_shapes=scratch,
        name=name,
        cost_estimate=pl.CostEstimate(
            flops=int(gflop * 1e9), bytes_accessed=1 << 20, transcendentals=0
        ),
        compiler_params=pltpu.CompilerParams(vmem_limit_bytes=limit << 20),
    )(*operands)


SHARE = 96


def turn_patches_body(pos, p, mine, send, t):
    pt = p[...].T
    for b in range(16):
        for half in range(2):
            at = (b * 2 + half) * 48
            t[b, half] = pt[at : at + 48]
    c = pos[3]
    mine[...] = t[:, c]
    send[...] = t[:, 1 - c]


def gelu_pass_body(
    pos, gain, p, g, stem_any, up_any, down_any,
    preact_grad, normal, inverse, mine, send,
    w, u, d, t, sem,
):
    plan = []
    for k in range(3):
        rows = pl.ds(k * 512, 512)
        plan.append((stem_any.at[rows], w.at[rows]))
    for k in range(2):
        cols = pl.ds(k * 1024, 1024)
        plan.append((up_any.at[:, cols], u.at[:, cols]))
        plan.append((down_any.at[cols], d.at[cols]))
    copies = [pltpu.make_async_copy(src, dst, sem.at[k]) for k, (src, dst) in enumerate(plan)]
    for copy in copies:
        copy.start()

    acc = None
    for k in range(3):
        copies[k].wait()
        part = jnp.dot(
            p[:, k * 512 : k * 512 + 512], w[k * 512 : k * 512 + 512], preferred_element_type=F32
        )
        acc = part if acc is None else acc + part
    embed = acc.astype(BF).astype(F32)
    center = jnp.mean(embed, axis=1, keepdims=True)
    shifted = embed - center
    scale = lax.rsqrt(jnp.mean(shifted * shifted, axis=1, keepdims=True) + 1e-06)
    norm = shifted * scale
    normal[...] = norm
    inverse[...] = scale
    normed = (norm * gain[...]).astype(BF)
    nt = normed.T
    for b in range(16):
        for half in range(2):
            at = b * 2 + half
            t[b, half, 64:96] = nt[at * 32 : at * 32 + 32]
    for j in range(8):
        if j % 4 == 0:
            copies[3 + j // 2].wait()
            copies[4 + j // 2].wait()
        cols = slice(j * 256, j * 256 + 256)
        pre = jnp.dot(normed, u[:, cols], preferred_element_type=F32)
        grad = lax.dot_general(g[...], d[cols], OVER_COLUMNS, preferred_element_type=F32)
        cdf = 0.5 * (1.0 + lax.erf(pre * math.sqrt(0.5)))
        slope = cdf + pre * jnp.exp(-0.5 * pre * pre) * (1.0 / math.sqrt(2.0 * math.pi))
        preact_grad[:, cols] = (grad * slope).astype(BF)
        ht = (pre * cdf).astype(BF).T
        for q in range(4):
            t[j * 2 + q // 2, q % 2, 0:64] = ht[q * 64 : q * 64 + 64]
    c = pos[3]
    mine[...] = t[:, c]
    send[...] = t[:, 1 - c]


def gelu_pass(pos, gain, patches, cotangent, stem_weight, up_weight, down_weight):
    outs = [((256, 2048), BF), ((256, 1024), F32), ((256, 1), F32)]
    return call(
        gelu_pass_body,
        outs + [((16, SHARE, 256), BF)] * 2,
        [
            pltpu.VMEM((1536, 1024), BF),
            pltpu.VMEM((1024, 2048), BF),
            pltpu.VMEM((2048, 1024), BF),
            pltpu.VMEM((16, 2, SHARE, 256), BF),
            pltpu.SemaphoreType.DMA((7,)),
        ],
        "gelu_pass",
        pos,
        gain,
        patches,
        cotangent,
        stem_weight,
        up_weight,
        down_weight,
        limit=48,
        specs=[SMEM] + [VMEM] * 3 + [pl.BlockSpec(memory_space=pl.ANY)] * 3,
        gflop=8,
    )


def norm_back_body(gain, preact_grad, up, cot, normal, inverse, embed_grad):
    grad = lax.dot_general(preact_grad[...], up[...], OVER_COLUMNS, preferred_element_type=F32)
    grad = grad * gain[...]
    norm = normal[...]
    first = jnp.mean(grad, axis=1, keepdims=True)
    second = jnp.mean(grad * norm, axis=1, keepdims=True)
    embed_grad[...] = (
        cot[...].astype(F32) + inverse[...] * (grad - first - norm * second)
    ).astype(BF)


ROWS = 176
SPLIT = 4
CHUNK_X = 512 + SPLIT * 64 + 32
CHUNK_Y = (8 - SPLIT) * 64 - 32 + 384


def up_rows(z, k):
    at = z * 64 + k * 32
    return ("x", 512 + at) if at < SPLIT * 64 + 32 else ("y", at - SPLIT * 64 - 32)


def chunk_of(me, pos, rel):
    return lax.rem(me + rel * (1 + 2 * pos[3]), 4)


def dot2(lefts, rights):
    left, right = jnp.concatenate(lefts, axis=1), jnp.concatenate(rights, axis=0)
    return jnp.dot(left, right, preferred_element_type=F32).astype(BF)


def columns(ref, starts, width):
    parts = [ref[:, pl.ds(pl.multiple_of(start, LANES), width)] for start in starts]
    return parts[0] if len(parts) == 1 else jnp.concatenate(parts, axis=1)


def terms_x_body(pos, lm, lr, cm, cr, gm, gr, *outs):
    for rel in range(4):
        to = chunk_of(pos[0], pos, rel)
        xh, xl = to // 2, lax.rem(to, 2)
        dst = outs[rel]
        acc = dot2(
            [ref[:, xh, 0:64].reshape(512, 256) for ref in (lm, lr)],
            [columns(ref, [xl * 512], 512) for ref in (cm, cr)],
        )
        for yy in range(4):
            dst[yy, 0:512] = acc[:, yy * 128 : yy * 128 + 128]
        acc = dot2(
            [ref[0 : SPLIT + 1, xh, 64:96].reshape(SPLIT * 32 + 32, 256) for ref in (lm, lr)],
            [columns(ref, [(yy * 2 + xl) * 256 for yy in range(4)], 256) for ref in (gm, gr)],
        )
        for z in range(SPLIT + 1):
            for k in range(2):
                part, at = up_rows(z, k)
                for yy in range(4 if part == "x" else 0):
                    col = (yy * 2 + k) * 128
                    dst[yy, at : at + 32] = acc[z * 32 : z * 32 + 32, col : col + 128]


def terms_y_body(pos, lm, lr, pm, pr, gm, gr, em, er, *outs):
    for rel in range(4):
        to = chunk_of(pos[1], pos, rel)
        dst = outs[rel]
        acc = dot2(
            [ref[SPLIT:8, :, 64:96].reshape((8 - SPLIT) * 64, 256) for ref in (lm, lr)],
            [columns(ref, [to * 512], 512) for ref in (gm, gr)],
        )
        for z in range(SPLIT, 8):
            for k in range(2):
                part, at = up_rows(z, k)
                for xx in range(4 if part == "y" else 0):
                    row, col = ((z - SPLIT) * 2 + xx // 2) * 32, (xx % 2 * 2 + k) * 128
                    dst[xx, at : at + 32] = acc[row : row + 32, col : col + 128]
        acc = dot2(
            [ref[...].reshape(768, 256) for ref in (pm, pr)],
            [columns(ref, [to * 128, 512 + to * 128], 128) for ref in (em, er)],
        )
        for z in range(8):
            for xx in range(4):
                row, col = (z * 2 + xx // 2) * 48, xx % 2 * 128
                at = CHUNK_Y - 384 + z * 48
                dst[xx, at : at + 48] = acc[row : row + 48, col : col + 128]


def pass_on_body(keep, got, out):
    out[...] = (keep[...].astype(F32) + got[...].astype(F32)).astype(BF)


def rings(axes, parts):
    result = []
    for p, (axis, (own, keep, ahead, behind)) in enumerate(zip(axes, parts)):
        got = move(ahead, axis, 1)
        near = move(behind, axis, -1)
        if p == 1:
            got, near = lax.optimization_barrier((got, near))
        (total,) = call(
            pass_on_body, [(keep.shape, BF)], [], "pass_on", keep, got, specs=[VMEM, VMEM]
        )
        result += [own, near, move(total, axis, 1)]
    return result


def add3(a, b, c):
    return (a.astype(F32) + b.astype(F32) + c.astype(F32)).astype(BF)


def turn_body(second, pos, own, near, far, *outs):
    for rel in range(4):
        to = chunk_of(pos[second], pos, rel)
        outs[rel][...] = add3(own[to], near[to], far[to])


def reduce_xy(pos, parts):
    sums = rings("xy", parts)
    turned = [
        call(
            functools.partial(turn_body, 1 - p),
            [(sums[3 * p].shape[1:], BF)] * 4,
            [],
            "ring_turn_" + "xy"[p],
            pos,
            *sums[3 * p : 3 * p + 3],
        )
        for p in range(2)
    ]
    return rings("yx", turned)


def pack_body(*refs):
    out = refs[6]
    x, y = (add3(*(ref[...] for ref in refs[3 * p : 3 * p + 3])) for p in range(2))
    for z in range(8):
        out[z, 0:64] = x[z * 64 : z * 64 + 64]
        for k in range(2):
            part, at = up_rows(z, k)
            up = x if part == "x" else y
            out[z, 64 + k * 32 : 96 + k * 32] = up[at : at + 32]
        at = CHUNK_Y - 384 + z * 48
        out[z, 128:176] = y[at : at + 48]


def sum_body(got, out):
    total = got[0].astype(F32)
    for k in range(1, 8):
        total += got[k].astype(F32)
    share = total.astype(BF)
    for k in range(8):
        out[k] = share


def unpack_body(got, stem, up, down):
    for y in range(4):
        for xl in range(2):
            piece = got[y * 2 + xl].astype(F32)
            col = (xl * 4 + y) * LANES
            down[:, col : col + LANES] = piece[0:64]
            stem[:, col : col + LANES] = piece[128:176]
            col = (y * 2 + xl) * 256
            up[:, col : col + LANES] = piece[64:96]
            up[:, col + LANES : col + 256] = piece[96:128]


def finish(pieces):
    share = [((8, ROWS, LANES), BF)]
    (packed,) = call(pack_body, share, [], "z_pack", *pieces, specs=[VMEM] * 6)
    got = lax.all_to_all(packed, "z", 0, 0, tiled=True)
    (copies,) = call(sum_body, share, [], "z_sum", got, specs=[VMEM])
    every = lax.all_to_all(copies, ("y", "xl"), 0, 0, tiled=True)
    outs = [((48, 1024), F32), ((32, 2048), F32), ((64, 1024), F32)]
    return call(unpack_body, outs, [], "unpack", every, specs=[VMEM])


def local(patches, stem_weight, ln_gain, up_weight, down_weight, cotangent):
    x = lax.axis_index("xh") * 2 + lax.axis_index("xl")
    pos = jnp.stack([x, lax.axis_index("y"), lax.axis_index("z"), lax.axis_index("c")])
    pos = pos.astype(jnp.int32)

    gain = ln_gain.reshape(1, 1024)
    patches_mine, patches_send = call(
        turn_patches_body,
        [((16, 48, 256), BF)] * 2,
        [pltpu.VMEM((16, 2, 48, 256), BF)],
        "turn_patches",
        pos,
        patches,
        limit=12,
        gflop=2,
    )
    patches_other = move(patches_send, "c", 0)
    cot_other = move(cotangent, "c", 0)
    preact_grad, normal, inverse, mine, send = gelu_pass(
        pos, gain, patches, cotangent, stem_weight, up_weight, down_weight
    )
    send, cot_other, patches_other = lax.optimization_barrier((send, cot_other, patches_other))
    other = move(send, "c", 0)
    preact_other = move(preact_grad, "c", 0)
    (embed_grad,) = call(
        norm_back_body,
        [((256, 1024), BF)],
        [],
        "norm_back",
        gain,
        preact_grad,
        up_weight,
        cotangent,
        normal,
        inverse,
        specs=[VMEM] * 6,
        limit=16,
        gflop=2,
    )
    embed_other = move(embed_grad, "c", 0)

    left = [v.reshape(8, 2, SHARE, 256) for v in (mine, other)]
    outs_x, outs_y = ([((4, rows, LANES), BF)] * 4 for rows in (CHUNK_X, CHUNK_Y))
    grads = (preact_grad, preact_other)
    part_x = call(
        terms_x_body, outs_x, [], "terms_x", pos, *left, cotangent, cot_other, *grads, limit=16, gflop=2
    )
    embed_other, *part_x = lax.optimization_barrier((embed_other, *part_x))
    part_y = call(
        terms_y_body, outs_y, [], "terms_y", pos, *left, patches_mine, patches_other, *grads, embed_grad, embed_other, limit=16, gflop=2
    )
    return tuple(finish(reduce_xy(pos, (part_x, part_y))))


def solution(mesh):
    fine = Mesh(mesh.devices.reshape(4, 2, 8, 2, 2), AXES)
    rows = P(("z", "xh", "c"), None)
    in_specs = (P(AXES, None), P(), P(), P(), P(), P(AXES, None))
    return jax.shard_map(
        local, mesh=fine, in_specs=in_specs, out_specs=(rows, rows, rows), check_vma=False
    )
```

```python
import functools
import math

import jax
import jax.numpy as jnp
from jax import lax
from jax.experimental import pallas as pl
from jax.experimental.pallas import tpu as pltpu
from jax.sharding import Mesh, PartitionSpec as P

BF = jnp.bfloat16
F32 = jnp.float32
AXES = ("y", "xl", "z", "xh", "c")
VMEM = pl.BlockSpec(memory_space=pltpu.VMEM)
SMEM = pl.BlockSpec(memory_space=pltpu.SMEM)
LANES = 128
OVER_COLUMNS = (((1,), (1,)), ((), ()))


def move(value, axis, hop):
    pairs = []
    for y in range(4):
        for x in range(4):
            for z in range(8):
                for c in range(2):
                    far = hop * (1 - 2 * c)
                    X = (x + far) % 4 if axis == "x" else x
                    Y = (y + far) % 4 if axis == "y" else y
                    C = 1 - c if axis == "c" else c
                    src = (y * 2 + x % 2) * 32 + z * 4 + (x // 2) * 2 + c
                    dst = (Y * 2 + X % 2) * 32 + z * 4 + (X // 2) * 2 + C
                    pairs.append((src, dst))
    return lax.ppermute(value, AXES, sorted(pairs))


def call(body, outs, scratch, name, *operands, limit=8, specs=None, gflop=0.02):
    return pl.pallas_call(
        body,
        out_shape=[jax.ShapeDtypeStruct(s, d) for s, d in outs],
        in_specs=specs or [SMEM] + [VMEM] * (len(operands) - 1),
        out_specs=[VMEM] * len(outs),
        scratch_shapes=scratch,
        name=name,
        cost_estimate=pl.CostEstimate(
            flops=int(gflop * 1e9), bytes_accessed=1 << 20, transcendentals=0
        ),
        compiler_params=pltpu.CompilerParams(vmem_limit_bytes=limit << 20),
    )(*operands)


SHARE = 96


def turn_patches_body(pos, p, mine, send, t):
    pt = p[...].T
    for b in range(16):
        for half in range(2):
            at = (b * 2 + half) * 48
            t[b, half] = pt[at : at + 48]
    c = pos[3]
    mine[...] = t[:, c]
    send[...] = t[:, 1 - c]


def gelu_pass_body(
    pos, gain, p, g, stem_any, up_any, down_any,
    preact_grad, normal, inverse, mine, send,
    w, u, d, t, sem,
):
    plan = []
    for k in range(3):
        rows = pl.ds(k * 512, 512)
        plan.append((stem_any.at[rows], w.at[rows]))
    for k in range(2):
        cols = pl.ds(k * 1024, 1024)
        plan.append((up_any.at[:, cols], u.at[:, cols]))
        plan.append((down_any.at[cols], d.at[cols]))
    copies = [pltpu.make_async_copy(src, dst, sem.at[k]) for k, (src, dst) in enumerate(plan)]
    for copy in copies:
        copy.start()

    acc = None
    for k in range(3):
        copies[k].wait()
        part = jnp.dot(
            p[:, k * 512 : k * 512 + 512], w[k * 512 : k * 512 + 512], preferred_element_type=F32
        )
        acc = part if acc is None else acc + part
    embed = acc.astype(BF).astype(F32)
    center = jnp.mean(embed, axis=1, keepdims=True)
    shifted = embed - center
    scale = lax.rsqrt(jnp.mean(shifted * shifted, axis=1, keepdims=True) + 1e-06)
    norm = shifted * scale
    normal[...] = norm
    inverse[...] = scale
    normed = (norm * gain[...]).astype(BF)
    nt = normed.T
    for b in range(16):
        for half in range(2):
            at = b * 2 + half
            t[b, half, 64:96] = nt[at * 32 : at * 32 + 32]
    for j in range(4):
        if j % 2 == 0:
            copies[3 + j].wait()
            copies[4 + j].wait()
        cols = slice(j * 512, j * 512 + 512)
        pre = jnp.dot(normed, u[:, cols], preferred_element_type=F32)
        grad = lax.dot_general(g[...], d[cols], OVER_COLUMNS, preferred_element_type=F32)
        cdf = 0.5 * (1.0 + lax.erf(pre * math.sqrt(0.5)))
        slope = cdf + pre * jnp.exp(-0.5 * pre * pre) * (1.0 / math.sqrt(2.0 * math.pi))
        preact_grad[:, cols] = (grad * slope).astype(BF)
        ht = (pre * cdf).astype(BF).T
        for q in range(8):
            t[j * 4 + q // 2, q % 2, 0:64] = ht[q * 64 : q * 64 + 64]
    c = pos[3]
    mine[...] = t[:, c]
    send[...] = t[:, 1 - c]


def gelu_pass(pos, gain, patches, cotangent, stem_weight, up_weight, down_weight):
    outs = [((256, 2048), BF), ((256, 1024), F32), ((256, 1), F32)]
    return call(
        gelu_pass_body,
        outs + [((16, SHARE, 256), BF)] * 2,
        [
            pltpu.VMEM((1536, 1024), BF),
            pltpu.VMEM((1024, 2048), BF),
            pltpu.VMEM((2048, 1024), BF),
            pltpu.VMEM((16, 2, SHARE, 256), BF),
            pltpu.SemaphoreType.DMA((7,)),
        ],
        "gelu_pass",
        pos,
        gain,
        patches,
        cotangent,
        stem_weight,
        up_weight,
        down_weight,
        limit=48,
        specs=[SMEM] + [VMEM] * 3 + [pl.BlockSpec(memory_space=pl.ANY)] * 3,
        gflop=8,
    )


def norm_back_body(gain, preact_grad, up, cot, normal, inverse, embed_grad):
    grad = lax.dot_general(preact_grad[...], up[...], OVER_COLUMNS, preferred_element_type=F32)
    grad = grad * gain[...]
    norm = normal[...]
    first = jnp.mean(grad, axis=1, keepdims=True)
    second = jnp.mean(grad * norm, axis=1, keepdims=True)
    embed_grad[...] = (
        cot[...].astype(F32) + inverse[...] * (grad - first - norm * second)
    ).astype(BF)


ROWS = 176
SPLIT = 4
CHUNK_X = 512 + SPLIT * 64 + 32
CHUNK_Y = (8 - SPLIT) * 64 - 32 + 384


def up_rows(z, k):
    at = z * 64 + k * 32
    return ("x", 512 + at) if at < SPLIT * 64 + 32 else ("y", at - SPLIT * 64 - 32)


def chunk_of(me, pos, rel):
    return lax.rem(me + rel * (1 + 2 * pos[3]), 4)


def dot2(lefts, rights):
    left, right = jnp.concatenate(lefts, axis=1), jnp.concatenate(rights, axis=0)
    return jnp.dot(left, right, preferred_element_type=F32).astype(BF)


def columns(ref, starts, width):
    parts = [ref[:, pl.ds(pl.multiple_of(start, LANES), width)] for start in starts]
    return parts[0] if len(parts) == 1 else jnp.concatenate(parts, axis=1)


def terms_x_body(pos, lm, lr, cm, cr, gm, gr, *outs):
    for rel in range(4):
        to = chunk_of(pos[0], pos, rel)
        xh, xl = to // 2, lax.rem(to, 2)
        dst = outs[rel]
        acc = dot2(
            [ref[:, xh, 0:64].reshape(512, 256) for ref in (lm, lr)],
            [columns(ref, [xl * 512], 512) for ref in (cm, cr)],
        )
        for yy in range(4):
            dst[yy, 0:512] = acc[:, yy * 128 : yy * 128 + 128]
        acc = dot2(
            [ref[0 : SPLIT + 1, xh, 64:96].reshape(SPLIT * 32 + 32, 256) for ref in (lm, lr)],
            [columns(ref, [(yy * 2 + xl) * 256 for yy in range(4)], 256) for ref in (gm, gr)],
        )
        for z in range(SPLIT + 1):
            for k in range(2):
                part, at = up_rows(z, k)
                for yy in range(4 if part == "x" else 0):
                    col = (yy * 2 + k) * 128
                    dst[yy, at : at + 32] = acc[z * 32 : z * 32 + 32, col : col + 128]


def terms_y_body(pos, lm, lr, pm, pr, gm, gr, em, er, *outs):
    for rel in range(4):
        to = chunk_of(pos[1], pos, rel)
        dst = outs[rel]
        acc = dot2(
            [ref[SPLIT:8, :, 64:96].reshape((8 - SPLIT) * 64, 256) for ref in (lm, lr)],
            [columns(ref, [to * 512], 512) for ref in (gm, gr)],
        )
        for z in range(SPLIT, 8):
            for k in range(2):
                part, at = up_rows(z, k)
                for xx in range(4 if part == "y" else 0):
                    row, col = ((z - SPLIT) * 2 + xx // 2) * 32, (xx % 2 * 2 + k) * 128
                    dst[xx, at : at + 32] = acc[row : row + 32, col : col + 128]
        acc = dot2(
            [ref[...].reshape(768, 256) for ref in (pm, pr)],
            [columns(ref, [to * 128, 512 + to * 128], 128) for ref in (em, er)],
        )
        for z in range(8):
            for xx in range(4):
                row, col = (z * 2 + xx // 2) * 48, xx % 2 * 128
                at = CHUNK_Y - 384 + z * 48
                dst[xx, at : at + 48] = acc[row : row + 48, col : col + 128]


def pass_on_body(keep, got, out):
    out[...] = (keep[...].astype(F32) + got[...].astype(F32)).astype(BF)


def rings(axes, parts):
    result = []
    for p, (axis, (own, keep, ahead, behind)) in enumerate(zip(axes, parts)):
        got = move(ahead, axis, 1)
        near = move(behind, axis, -1)
        if p == 1:
            got, near = lax.optimization_barrier((got, near))
        (total,) = call(
            pass_on_body, [(keep.shape, BF)], [], "pass_on", keep, got, specs=[VMEM, VMEM]
        )
        result += [own, near, move(total, axis, 1)]
    return result


def add3(a, b, c):
    return (a.astype(F32) + b.astype(F32) + c.astype(F32)).astype(BF)


def turn_body(second, pos, own, near, far, *outs):
    for rel in range(4):
        to = chunk_of(pos[second], pos, rel)
        outs[rel][...] = add3(own[to], near[to], far[to])


def reduce_xy(pos, parts):
    sums = rings("xy", parts)
    turned = [
        call(
            functools.partial(turn_body, 1 - p),
            [(sums[3 * p].shape[1:], BF)] * 4,
            [],
            "ring_turn_" + "xy"[p],
            pos,
            *sums[3 * p : 3 * p + 3],
        )
        for p in range(2)
    ]
    return rings("yx", turned)


def pack_body(*refs):
    out = refs[6]
    x, y = (add3(*(ref[...] for ref in refs[3 * p : 3 * p + 3])) for p in range(2))
    for z in range(8):
        out[z, 0:64] = x[z * 64 : z * 64 + 64]
        for k in range(2):
            part, at = up_rows(z, k)
            up = x if part == "x" else y
            out[z, 64 + k * 32 : 96 + k * 32] = up[at : at + 32]
        at = CHUNK_Y - 384 + z * 48
        out[z, 128:176] = y[at : at + 48]


def sum_body(got, out):
    total = got[0].astype(F32)
    for k in range(1, 8):
        total += got[k].astype(F32)
    share = total.astype(BF)
    for k in range(8):
        out[k] = share


def unpack_body(got, stem, up, down):
    for y in range(4):
        for xl in range(2):
            piece = got[y * 2 + xl].astype(F32)
            col = (xl * 4 + y) * LANES
            down[:, col : col + LANES] = piece[0:64]
            stem[:, col : col + LANES] = piece[128:176]
            col = (y * 2 + xl) * 256
            up[:, col : col + LANES] = piece[64:96]
            up[:, col + LANES : col + 256] = piece[96:128]


def finish(pieces):
    share = [((8, ROWS, LANES), BF)]
    (packed,) = call(pack_body, share, [], "z_pack", *pieces, specs=[VMEM] * 6)
    got = lax.all_to_all(packed, "z", 0, 0, tiled=True)
    (copies,) = call(sum_body, share, [], "z_sum", got, specs=[VMEM])
    every = lax.all_to_all(copies, ("y", "xl"), 0, 0, tiled=True)
    outs = [((48, 1024), F32), ((32, 2048), F32), ((64, 1024), F32)]
    return call(unpack_body, outs, [], "unpack", every, specs=[VMEM])


def local(patches, stem_weight, ln_gain, up_weight, down_weight, cotangent):
    x = lax.axis_index("xh") * 2 + lax.axis_index("xl")
    pos = jnp.stack([x, lax.axis_index("y"), lax.axis_index("z"), lax.axis_index("c")])
    pos = pos.astype(jnp.int32)

    gain = ln_gain.reshape(1, 1024)
    patches_mine, patches_send = call(
        turn_patches_body,
        [((16, 48, 256), BF)] * 2,
        [pltpu.VMEM((16, 2, 48, 256), BF)],
        "turn_patches",
        pos,
        patches,
        limit=12,
        gflop=2,
    )
    patches_other = move(patches_send, "c", 0)
    cot_other = move(cotangent, "c", 0)
    preact_grad, normal, inverse, mine, send = gelu_pass(
        pos, gain, patches, cotangent, stem_weight, up_weight, down_weight
    )
    send, cot_other, patches_other = lax.optimization_barrier((send, cot_other, patches_other))
    other = move(send, "c", 0)
    preact_other = move(preact_grad, "c", 0)
    (embed_grad,) = call(
        norm_back_body,
        [((256, 1024), BF)],
        [],
        "norm_back",
        gain,
        preact_grad,
        up_weight,
        cotangent,
        normal,
        inverse,
        specs=[VMEM] * 6,
        limit=16,
        gflop=2,
    )
    embed_other = move(embed_grad, "c", 0)

    left = [v.reshape(8, 2, SHARE, 256) for v in (mine, other)]
    outs_x, outs_y = ([((4, rows, LANES), BF)] * 4 for rows in (CHUNK_X, CHUNK_Y))
    grads = (preact_grad, preact_other)
    part_x = call(
        terms_x_body, outs_x, [], "terms_x", pos, *left, cotangent, cot_other, *grads, limit=16, gflop=2
    )
    embed_other, *part_x = lax.optimization_barrier((embed_other, *part_x))
    part_y = call(
        terms_y_body, outs_y, [], "terms_y", pos, *left, patches_mine, patches_other, *grads, embed_grad, embed_other, limit=16, gflop=2
    )
    return tuple(finish(reduce_xy(pos, (part_x, part_y))))


def solution(mesh):
    fine = Mesh(mesh.devices.reshape(4, 2, 8, 2, 2), AXES)
    rows = P(("z", "xh", "c"), None)
    in_specs = (P(AXES, None), P(), P(), P(), P(), P(AXES, None))
    return jax.shard_map(
        local, mesh=fine, in_specs=in_specs, out_specs=(rows, rows, rows), check_vma=False
    )
```
